128 devices in a mesh: sample: 4 (over x_lo, core), tok: 32 (over x_hi, y, z).
Axes of the slice: x: 4 (x_hi: 2, x_lo: 2; x = x_hi * 2 + x_lo), y: 4, z: 4, core: 2. Of those that a mesh axis runs over, the one named last changes fastest.
Arguments:
- atom_cond: bfloat16 [49152, 128], P('tok'), may hold values from -6 to 6
- atom_pos: float32 [16, 3, 49152], P('sample', None, 'tok'), may hold values from -6 to 6
- atom_token: int32 [49152], P('tok'), may hold values from 0 to 64, as said below
- pos_weight: float32 [3, 128], replicated, may hold values from -4 to 4
- atom_proj: bfloat16 [128, 384], replicated, may hold values from -10 to 10
- atom_output: bfloat16 [128, 128], replicated, may hold values from -0.5 to 0.5
- atom_to_token: bfloat16 [128, 768], replicated, may hold values from -0.5 to 0.5
- tok_single: bfloat16 [2048, 768], P('tok'), may hold values from -6 to 6
- ada_weight: bfloat16 [768, 768], replicated, may hold values from -0.21875 to 0.21875
- pair_rep: bfloat16 [2048, 2048, 128], P('tok', 'sample'), may hold values from -6 to 6
- pair_weight: bfloat16 [128, 16], replicated, may hold values from -0.5 to 0.5
- tok_proj: bfloat16 [768, 3072], replicated, may hold values from -8 to 8
- tok_output: bfloat16 [768, 768], replicated, may hold values from -0.21875 to 0.21875
- transition_in: bfloat16 [768, 3072], replicated, may hold values from -0.21875 to 0.21875
- transition_out: bfloat16 [1536, 768], replicated, may hold values from -0.15625 to 0.15625
- token_to_atom: bfloat16 [768, 128], replicated, may hold values from -0.21875 to 0.21875
- pos_update: float32 [128, 3], replicated, may hold values from -0.5 to 0.5
Outputs:
- token_out: bfloat16 [16, 2048, 768], P('sample', 'tok')
- atom_update: float32 [16, 3, 49152], P('sample', None, 'tok')
The draws below stay inside these ranges and needn't reach their ends.
Inputs may be any that keep to these rules, and one draw needn't show every extreme that they name: `atom_token`: entry l gives the position, among the 64 tokens of block l // 1536, of the token of slot l; 64 marks an empty slot. Within a block the slots of a token are consecutive, tokens stand in order, empty slots come last, and every token has 4 to 24 slots. Some blocks are full.
All inputs are finite; a program needn't handle non-finite values.
Results may differ from the reference program's by a relative error of at most 0.035.
Values may be sent and summed in bfloat16 or wider, within the bound.
No kernel may reach another device: no remote copies, remote signals or barrier semaphores. Data moves between devices by JAX's collectives and lax.ppermute only.
A program may use at most 256 MiB of HBM per device.

```python
import jax
import jax.numpy as jnp
import numpy as np
from jax import lax

TOK_WIDTH = 768
TOK_HEADS = 16
PAIR_WIDTH = 128
ATOM_WIDTH = 128
ATOM_HEADS = 4
QUERY_BLOCK = 32
KEY_WINDOW = 128
MEAN_ATOMS = 8
TOK_DEV = 64
FF_WIDTH = 1536
ATOM_DEV = 1536
TOKENS = 2048
ALL_ATOMS = 49152
SAMPLES = 16
N_TOK = 32


def draw_atom_token(key, part):
    key = jax.random.fold_in(key, 7)
    pick_key, dense_key, count_key = jax.random.split(key, 3)
    block_count = ALL_ATOMS // ATOM_DEV
    chosen = jax.random.randint(pick_key, (), 0, block_count)
    dense = (jax.random.randint(dense_key, (block_count,), 0, 8) == 0) | (jnp.arange(block_count) == chosen)
    counts = jax.random.randint(count_key, (block_count, TOK_DEV), MEAN_ATOMS // 2, 3 * MEAN_ATOMS // 2 + 1)
    counts = jnp.where(dense[:, None], 3 * MEAN_ATOMS, counts)
    ends = jnp.cumsum(counts, axis=1)
    slots = jnp.arange(ATOM_DEV)
    owner = jnp.sum((ends[:, :, None] <= slots[None, None, :]).astype(jnp.int32), axis=1)
    return owner.reshape(-1).astype(jnp.int32)


def draw_atom_proj(key, part):
    key = jax.random.fold_in(key, 13)
    base = jax.random.truncated_normal(key, -4.0, 4.0, (ATOM_WIDTH, 3 * ATOM_WIDTH), jnp.float32) * ATOM_WIDTH ** (-0.5)
    return base.astype(jnp.bfloat16)


def draw_tok_proj(key, part):
    key = jax.random.fold_in(key, 19)
    base = jax.random.truncated_normal(key, -4.0, 4.0, (TOK_WIDTH, 4 * TOK_WIDTH), jnp.float32) * TOK_WIDTH ** (-0.5)
    return base.astype(jnp.bfloat16)


def block_levels(rng, extent, cuts, least, largest):
    gain = 1.0
    for dim, parts in cuts:
        steps = jax.random.uniform(jax.random.fold_in(jax.random.fold_in(rng, 6), dim), (parts,), jnp.float32, least / len(cuts), largest / len(cuts))
        gain = gain * jnp.repeat(jnp.exp(steps), extent[dim] // parts).reshape((-1,) + (1,) * (len(extent) - 1 - dim))
    return gain


def noise(own_key, dims, width, limit, shards=(), dtype=jnp.bfloat16):
    values = jax.random.normal(own_key, dims, jnp.float32) * width
    if len(shards) > 0:
        values = block_levels(own_key, dims, shards, -0.22, 0.18) * values
    return jnp.clip(values, min=-limit, max=limit).astype(dtype)


def setup_inputs(seed: int = 0) -> dict:
    key_of = jax.random.split(jax.random.key(seed), 18)
    return {
        "atom_cond": noise(key_of[0], (ALL_ATOMS, ATOM_WIDTH), 1.0, 6.0, ((0, 32),)),
        "atom_pos": noise(key_of[1], (SAMPLES, 3, ALL_ATOMS), 1.0, 6.0, ((0, 4), (2, 32)), jnp.float32),
        "atom_token": draw_atom_token(jax.random.fold_in(key_of[17], 71), 0),
        "pos_weight": noise(key_of[3], (3, ATOM_WIDTH), 0.6, 4.0, (), jnp.float32),
        "atom_proj": draw_atom_proj(jax.random.fold_in(key_of[17], 71), 0),
        "atom_output": noise(key_of[5], (ATOM_WIDTH, ATOM_WIDTH), ATOM_WIDTH ** -0.5, 0.5),
        "atom_to_token": noise(key_of[6], (ATOM_WIDTH, TOK_WIDTH), ATOM_WIDTH ** -0.5, 0.5),
        "tok_single": noise(key_of[7], (TOKENS, TOK_WIDTH), 1.0, 6.0, ((0, 32),)),
        "ada_weight": noise(key_of[8], (TOK_WIDTH, TOK_WIDTH), TOK_WIDTH ** -0.5, 0.21875),
        "pair_rep": noise(key_of[9], (TOKENS, TOKENS, PAIR_WIDTH), 1.0, 6.0, ((0, 32), (1, 4))),
        "pair_weight": noise(key_of[10], (PAIR_WIDTH, TOK_HEADS), PAIR_WIDTH ** -0.5, 0.5),
        "tok_proj": draw_tok_proj(jax.random.fold_in(key_of[17], 71), 0),
        "tok_output": noise(key_of[12], (TOK_WIDTH, TOK_WIDTH), TOK_WIDTH ** -0.5, 0.21875),
        "transition_in": noise(key_of[13], (TOK_WIDTH, 2 * FF_WIDTH), TOK_WIDTH ** -0.5, 0.21875),
        "transition_out": noise(key_of[14], (FF_WIDTH, TOK_WIDTH), FF_WIDTH ** -0.5, 0.15625),
        "token_to_atom": noise(key_of[15], (TOK_WIDTH, ATOM_WIDTH), TOK_WIDTH ** -0.5, 0.21875),
        "pos_update": noise(key_of[16], (ATOM_WIDTH, 3), ATOM_WIDTH ** -0.5, 0.5, (), jnp.float32),
    }


NORM_EPSILON = 1e-05
MASKED_SCORE = -1000000000.0

def layer_norm(inputs):
    row_mean = lax.optimization_barrier(jnp.mean(inputs, axis=-1, keepdims=True))
    centered = inputs - row_mean
    variance = lax.optimization_barrier(jnp.mean(centered * centered, axis=-1, keepdims=True))
    return centered * lax.rsqrt(variance + NORM_EPSILON)

def window_table(slot_count):
    starts = np.clip(np.arange(slot_count // QUERY_BLOCK) * QUERY_BLOCK - (KEY_WINDOW - QUERY_BLOCK) // 2, 0, slot_count - KEY_WINDOW)
    return starts[:, None] + np.arange(KEY_WINDOW)[None, :]

def atom_window(atom_normed, atom_proj, filled):
    samples, slot_count, channels = atom_normed.shape
    head_size = channels // ATOM_HEADS
    blocks = slot_count // QUERY_BLOCK
    projected = jnp.einsum('sac,cf->saf', atom_normed.astype(jnp.float32), atom_proj.astype(jnp.float32))
    queries = projected[..., :channels].astype(jnp.bfloat16)
    key_rows = projected[..., channels:2 * channels].astype(jnp.bfloat16)
    val_rows = projected[..., 2 * channels:].astype(jnp.bfloat16)
    indices = window_table(slot_count)
    query_heads = queries.astype(jnp.float32).reshape(samples, blocks, QUERY_BLOCK, ATOM_HEADS, head_size)
    key_heads = key_rows[:, indices].astype(jnp.float32).reshape(samples, blocks, KEY_WINDOW, ATOM_HEADS, head_size)
    val_heads = val_rows[:, indices].astype(jnp.float32).reshape(samples, blocks, KEY_WINDOW, ATOM_HEADS, head_size)
    scores = jnp.einsum('sbqhd,sbkhd->sbhqk', query_heads, key_heads) * head_size ** (-0.5)
    scores = jnp.where(filled[indices][None, :, None, None, :], scores, MASKED_SCORE)
    row_top = lax.optimization_barrier(jnp.max(scores, axis=-1, keepdims=True))
    weights = jnp.exp(scores - row_top)
    row_total = lax.optimization_barrier(jnp.sum(weights, axis=-1, keepdims=True))
    rounded = lax.optimization_barrier(weights.astype(jnp.bfloat16)).astype(jnp.float32)
    weighted = jnp.einsum('sbhqk,sbkhd->sbhqd', rounded, val_heads) / row_total
    return weighted.transpose(0, 1, 3, 2, 4).reshape(samples, slot_count, channels).astype(jnp.bfloat16)

def reference(atom_cond, atom_pos, atom_token, pos_weight, atom_proj, atom_output, atom_to_token, tok_single, ada_weight, pair_rep, pair_weight, tok_proj, tok_output, transition_in, transition_out, token_to_atom, pos_update):
    cond_blocks = atom_cond.reshape(N_TOK, ATOM_DEV, ATOM_WIDTH)
    pos_blocks = atom_pos.reshape(SAMPLES, 3, N_TOK, ATOM_DEV).transpose(2, 0, 1, 3)
    slot_blocks = atom_token.reshape(N_TOK, ATOM_DEV)

    def encode(inputs):
        cond_rows, pos_rows, slot_tokens = inputs
        filled = slot_tokens < TOK_DEV
        onehot = (jnp.arange(TOK_DEV)[:, None] == slot_tokens[None, :]).astype(jnp.float32)
        atom_act = cond_rows.astype(jnp.float32)[None] + jnp.einsum('sca,cw->saw', pos_rows, pos_weight, precision=lax.Precision.HIGHEST)
        atom_normed = layer_norm(atom_act).astype(jnp.bfloat16)
        atom_mixed = atom_window(atom_normed, atom_proj, filled)
        atom_mid = atom_act + jnp.einsum('saw,wv->sav', atom_mixed.astype(jnp.float32), atom_output.astype(jnp.float32))
        mid_rounded = lax.optimization_barrier(atom_mid.astype(jnp.bfloat16)).astype(jnp.float32)
        atom_feature = jax.nn.relu(jnp.einsum('saw,wc->sac', mid_rounded, atom_to_token.astype(jnp.float32))).astype(jnp.bfloat16)
        summed = jnp.einsum('ta,sac->stc', onehot, atom_feature.astype(jnp.float32))
        members = lax.optimization_barrier(jnp.sum(onehot, axis=1))
        return (atom_mid, summed / members[None, :, None])
    middles, token_parts = lax.map(encode, (cond_blocks, pos_blocks, slot_blocks))
    token_in = token_parts.transpose(1, 0, 2, 3).reshape(SAMPLES, TOKENS, TOK_WIDTH)
    conditioning = jnp.dot(tok_single, ada_weight, preferred_element_type=jnp.float32)
    adapted = (layer_norm(token_in) * (1.0 + conditioning)[None]).astype(jnp.bfloat16)
    projected = jnp.einsum('stc,cf->stf', adapted.astype(jnp.float32), tok_proj.astype(jnp.float32))
    queries = projected[..., :TOK_WIDTH].astype(jnp.bfloat16)
    key_rows = projected[..., TOK_WIDTH:2 * TOK_WIDTH].astype(jnp.bfloat16)
    val_rows = projected[..., 2 * TOK_WIDTH:3 * TOK_WIDTH].astype(jnp.bfloat16)
    gating = jax.nn.sigmoid(projected[..., 3 * TOK_WIDTH:])

    def bias_rows(rows):
        pair_normed = layer_norm(rows.astype(jnp.float32)).astype(jnp.bfloat16)
        return jnp.einsum('ijc,ch->hij', pair_normed.astype(jnp.float32), pair_weight.astype(jnp.float32)).astype(jnp.bfloat16)
    bias_blocks = lax.map(bias_rows, pair_rep.reshape(N_TOK, TOK_DEV, TOKENS, PAIR_WIDTH))
    head_size = TOK_WIDTH // TOK_HEADS

    def attend_sample(inputs):
        query_rows, key_all, val_all = inputs
        key_heads = key_all.astype(jnp.float32).reshape(TOKENS, TOK_HEADS, head_size)
        val_heads = val_all.astype(jnp.float32).reshape(TOKENS, TOK_HEADS, head_size)

        def attend_block(block_in):
            query_block, bias_block = block_in
            query_heads = query_block.astype(jnp.float32).reshape(TOK_DEV, TOK_HEADS, head_size)
            scores = jnp.einsum('qhd,khd->hqk', query_heads, key_heads) * head_size ** (-0.5) + bias_block.astype(jnp.float32)
            row_top = lax.optimization_barrier(jnp.max(scores, axis=-1, keepdims=True))
            weights = jnp.exp(scores - row_top)
            row_total = lax.optimization_barrier(jnp.sum(weights, axis=-1, keepdims=True))
            rounded = lax.optimization_barrier(weights.astype(jnp.bfloat16)).astype(jnp.float32)
            weighted = jnp.einsum('hqk,khd->hqd', rounded, val_heads) / row_total
            return weighted.transpose(1, 0, 2).reshape(TOK_DEV, TOK_WIDTH)
        return lax.map(attend_block, (query_rows.reshape(N_TOK, TOK_DEV, TOK_WIDTH), bias_blocks)).reshape(TOKENS, TOK_WIDTH)
    attended = lax.map(attend_sample, (queries, key_rows, val_rows))
    gated_out = (gating * attended).astype(jnp.bfloat16)
    after_attn = token_in + jnp.einsum('stc,cf->stf', gated_out.astype(jnp.float32), tok_output.astype(jnp.float32))
    hidden_in = layer_norm(after_attn).astype(jnp.bfloat16)
    expanded = jnp.einsum('stc,cf->stf', hidden_in.astype(jnp.float32), transition_in.astype(jnp.float32))
    hidden = (jax.nn.silu(expanded[..., :FF_WIDTH]) * expanded[..., FF_WIDTH:]).astype(jnp.bfloat16)
    token_out = (after_attn + jnp.einsum('stf,fc->stc', hidden.astype(jnp.float32), transition_out.astype(jnp.float32))).astype(jnp.bfloat16)
    tok_feature = jnp.einsum('stc,cw->stw', token_out.astype(jnp.float32), token_to_atom.astype(jnp.float32)).astype(jnp.bfloat16)
    feature_blocks = tok_feature.reshape(SAMPLES, N_TOK, TOK_DEV, ATOM_WIDTH).transpose(1, 0, 2, 3)

    def decode(inputs):
        atom_mid, features, slot_tokens = inputs
        onehot = (jnp.arange(TOK_DEV)[:, None] == slot_tokens[None, :]).astype(jnp.float32)
        atom_final = atom_mid + jnp.einsum('ta,stw->saw', onehot, features.astype(jnp.float32))
        update = jnp.einsum('saw,wp->spa', layer_norm(atom_final), pos_update, precision=lax.Precision.HIGHEST)
        return update * (slot_tokens < TOK_DEV).astype(jnp.float32)[None, None, :]
    updates = lax.map(decode, (middles, feature_blocks, slot_blocks))
    atom_update = updates.transpose(1, 2, 0, 3).reshape(SAMPLES, 3, ALL_ATOMS)
    return (token_out, atom_update)
```

```python
import functools

import jax
import jax.numpy as jnp
import numpy as np
from jax import lax
from jax.experimental import pallas as pl
from jax.experimental.pallas import tpu as pltpu
from jax.sharding import Mesh, PartitionSpec as P

ATOM_HEADS = 4
QUERY_BLOCK = 32
KEY_WINDOW = 128
NORM_EPSILON = 1e-05
MASKED_SCORE = -1000000000.0
LOG2E = 1.4426950408889634
F32 = jnp.float32
BF16 = jnp.bfloat16
VMEM_LIMIT = 50 * 1024 * 1024

TN = (((0,), (0,)), ((), ()))
NT = (((1,), (1,)), ((), ()))
NN = (((1,), (0,)), ((), ()))


def mm(a, b, dims=NN):
    return lax.dot_general(a, b, dims, preferred_element_type=F32)


def norm_rows(inputs):
    row_mean = jnp.mean(inputs, axis=-1, keepdims=True)
    centered = inputs - row_mean
    variance = jnp.mean(centered * centered, axis=-1, keepdims=True)
    return centered * lax.rsqrt(variance + NORM_EPSILON)


def params():
    return pltpu.CompilerParams(vmem_limit_bytes=VMEM_LIMIT)


def pair_kernel(pair_ref, center_ref, weight_ref, out_ref):
    rows, cols, width = pair_ref.shape
    heads = weight_ref.shape[0]
    ones = jnp.full((heads, width), 1.0 / width, BF16)
    flat = pair_ref[...].reshape(rows * cols, width)
    centered = mm(flat, center_ref[...])
    top = mm(weight_ref[...], centered.astype(BF16), NT)
    variance = mm(ones, (centered * centered).astype(BF16), NT)
    bias = top * (lax.rsqrt(variance + NORM_EPSILON) * LOG2E)
    for h in range(heads):
        out_ref[h] = bias[h : h + 1].reshape(rows, cols).astype(BF16)


def pair_bias(pair_rep, pair_weight):
    rows, cols, width = pair_rep.shape
    heads = pair_weight.shape[1]
    step = 16
    center = jnp.asarray(np.eye(width) - 1.0 / width, BF16)
    return pl.pallas_call(
        pair_kernel,
        grid=(rows // step,),
        in_specs=[
            pl.BlockSpec((step, cols, width), lambda i: (i, 0, 0)),
            pl.BlockSpec((width, width), lambda i: (0, 0)),
            pl.BlockSpec((heads, width), lambda i: (0, 0)),
        ],
        out_specs=pl.BlockSpec((heads, step, cols), lambda i: (0, i, 0)),
        out_shape=jax.ShapeDtypeStruct((heads, rows, cols), BF16),
        compiler_params=params(),
        cost_estimate=pl.CostEstimate(
            flops=2 * rows * cols * width * (width + 2 * heads),
            bytes_accessed=2 * rows * cols * (width + heads),
            transcendentals=0,
        ),
        name="pair_bias",
    )(pair_rep, center, pair_weight.T)


def atom_kernel(
    cond_ref, pos_ref, token_ref, pos_weight_ref, proj_ref, output_ref, to_token_ref,
    mid_ref, token_in_ref, query_s, key_s, val_s, mixed_s,
):
    slots, width = cond_ref.shape
    tokens = token_in_ref.shape[1]
    head = width // ATOM_HEADS
    owner = token_ref[...]
    count = jnp.sum((owner < tokens).astype(jnp.int32))
    act = cond_ref[...].astype(F32) + lax.dot_general(
        pos_ref[0], pos_weight_ref[...], TN, precision=lax.Precision.HIGHEST, preferred_element_type=F32
    )
    normed = norm_rows(act).astype(BF16)
    projected = mm(normed, proj_ref[...])
    query_s[...] = (projected[:, :width] * (head ** (-0.5) * LOG2E)).astype(BF16)
    key_s[...] = projected[:, width : 2 * width].astype(BF16)
    val_s[:, :width] = projected[:, 2 * width :].astype(BF16)
    val_s[:, width:] = jnp.ones((slots, width), BF16)
    stacked = ATOM_HEADS * QUERY_BLOCK
    of_row = lax.broadcasted_iota(jnp.int32, (stacked, width), 0) // QUERY_BLOCK
    of_lane = lax.broadcasted_iota(jnp.int32, (stacked, width), 1) // head
    own_head = of_row == of_lane
    lane = lax.broadcasted_iota(jnp.int32, (stacked, KEY_WINDOW), 1)
    blocks = slots // QUERY_BLOCK
    group = 8
    for first in range(0, blocks, group):
        starts = [
            min(max(b * QUERY_BLOCK - (KEY_WINDOW - QUERY_BLOCK) // 2, 0), slots - KEY_WINDOW)
            for b in range(first, first + group)
        ]
        scores = []
        for k, start in enumerate(starts):
            low = (first + k) * QUERY_BLOCK
            query = query_s[low : low + QUERY_BLOCK, :]
            query = jnp.concatenate([query] * ATOM_HEADS, axis=0)
            query = jnp.where(own_head, query, jnp.zeros_like(query))
            score = mm(query, key_s[start : start + KEY_WINDOW, :], NT)
            scores.append(jnp.where(lane < count - start, score, MASKED_SCORE))
        weights = [jnp.exp2(s - jnp.max(s, axis=-1, keepdims=True)).astype(BF16) for s in scores]
        for k, start in enumerate(starts):
            low = (first + k) * QUERY_BLOCK
            summed = mm(weights[k], val_s[start : start + KEY_WINDOW, :])
            mixed = jnp.where(own_head, summed[:, :width] / summed[:, width:], 0.0)
            mixed = mixed.reshape(ATOM_HEADS, QUERY_BLOCK, width).sum(axis=0)
            mixed_s[low : low + QUERY_BLOCK, :] = mixed.astype(BF16)
    mid = act + mm(mixed_s[...], output_ref[...])
    mid_ref[0] = mid
    feature = jnp.maximum(mm(mid.astype(BF16), to_token_ref[...]), 0.0).astype(BF16)
    onehot = lax.broadcasted_iota(jnp.int32, (tokens, slots), 0) == owner
    members = jnp.sum(onehot.astype(F32), axis=1, keepdims=True)
    token_in_ref[0] = mm(onehot.astype(BF16), feature) / members


def atom_stage(atom_cond, atom_pos, atom_token, pos_weight, atom_proj, atom_output, atom_to_token, tokens):
    samples = atom_pos.shape[0]
    slots, width = atom_cond.shape
    channels = atom_to_token.shape[1]
    whole = lambda a: pl.BlockSpec(a.shape, lambda s: (0,) * a.ndim)
    atom_token = atom_token.reshape(1, slots)
    return pl.pallas_call(
        atom_kernel,
        grid=(samples,),
        in_specs=[
            whole(atom_cond),
            pl.BlockSpec((1, 3, slots), lambda s: (s, 0, 0)),
            whole(atom_token),
            whole(pos_weight),
            whole(atom_proj),
            whole(atom_output),
            whole(atom_to_token),
        ],
        out_specs=[
            pl.BlockSpec((1, slots, width), lambda s: (s, 0, 0)),
            pl.BlockSpec((1, tokens, channels), lambda s: (s, 0, 0)),
        ],
        out_shape=[
            jax.ShapeDtypeStruct((samples, slots, width), F32),
            jax.ShapeDtypeStruct((samples, tokens, channels), F32),
        ],
        scratch_shapes=[
            pltpu.VMEM((slots, width), BF16),
            pltpu.VMEM((slots, width), BF16),
            pltpu.VMEM((slots, 2 * width), BF16),
            pltpu.VMEM((slots, width), BF16),
        ],
        compiler_params=params(),
        cost_estimate=pl.CostEstimate(flops=20 * 10**9, bytes_accessed=10**7, transcendentals=10**7),
        name="atom_stage",
    )(atom_cond, atom_pos, atom_token, pos_weight, atom_proj, atom_output, atom_to_token)


def project_kernel(token_in_ref, single_ref, ada_ref, proj_ref, heads_ref, gate_ref):
    samples, tokens, channels = token_in_ref.shape
    heads, _, lanes = heads_ref.shape
    head = channels // heads
    conditioning = 1.0 + mm(single_ref[...], ada_ref[...])
    adapted = (norm_rows(token_in_ref[...]) * conditioning[None]).astype(BF16).reshape(lanes, channels)
    for part in range(3):
        rows = mm(adapted, proj_ref[:, part * channels : (part + 1) * channels])
        if part == 0:
            rows = rows * (head ** (-0.5) * LOG2E)
        turned = rows.T.astype(BF16).reshape(heads, head, lanes)
        heads_ref[:, part * head : (part + 1) * head, :] = turned
    gate = mm(adapted, proj_ref[:, 3 * channels :])
    gate_ref[...] = jax.nn.sigmoid(gate)


def project(token_in, tok_single, ada_weight, tok_proj, heads):
    samples, tokens, channels = token_in.shape
    lanes = samples * tokens
    head = channels // heads
    return pl.pallas_call(
        project_kernel,
        out_shape=[
            jax.ShapeDtypeStruct((heads, 3 * head, lanes), BF16),
            jax.ShapeDtypeStruct((lanes, channels), F32),
        ],
        compiler_params=params(),
        cost_estimate=pl.CostEstimate(
            flops=2 * lanes * channels * 4 * channels, bytes_accessed=8 * 10**6, transcendentals=lanes * channels
        ),
        name="project",
    )(token_in, tok_single, ada_weight, tok_proj)


def attend_kernel(
    order_ref, own_ref, far_ref, bias0_ref, bias1_ref, bias2_ref, bias3_ref, out_ref, query_s, key_s, val_s
):
    peers, head, lanes = out_ref.shape[0], out_ref.shape[1], out_ref.shape[2]
    samples = query_s.shape[0]
    tokens = lanes // samples
    width = query_s.shape[2]
    sources = own_ref.shape[0]
    half = sources * tokens
    step = pl.program_id(0)
    mine = order_ref[0]
    x_hi = order_ref[1]

    @pl.when(step == 0)
    def _():
        fill = jnp.zeros((width - head, lanes), F32)
        fill_v = jnp.where(lax.broadcasted_iota(jnp.int32, (width - head, lanes), 0) == 0, 1.0, 0.0)

        def turn(block, below):
            return jnp.concatenate([block.astype(F32), below], axis=0).T.astype(BF16)

        for j in range(sources):
            query = turn(own_ref[j, :head, :], fill)
            for s in range(samples):
                query_s[s, j * tokens : (j + 1) * tokens, :] = query[s * tokens : (s + 1) * tokens]
            for ref, low, which in ((own_ref, head, x_hi), (far_ref, 0, 1 - x_hi)):
                key = turn(ref[j, low : low + head, :], fill)
                val = turn(ref[j, low + head : low + 2 * head, :], fill_v)
                place = pl.ds(pl.multiple_of(which * half + j * tokens, tokens), tokens)
                for s in range(samples):
                    key_s[s, place, :] = key[s * tokens : (s + 1) * tokens]
                    val_s[s, place, :] = val[s * tokens : (s + 1) * tokens]

    rows = peers * tokens
    results = []
    for s in range(samples):
        query = query_s[s, pl.ds(pl.multiple_of(step * rows, rows), rows), :]
        scores = []
        places = []
        for p, bias_ref in enumerate((bias0_ref, bias1_ref, bias2_ref, bias3_ref)):
            cols = bias_ref.shape[1]
            place = pl.ds(pl.multiple_of((mine ^ p) * cols, cols), cols)
            places.append(place)
            scores.append(mm(query, key_s[s, place, :], NT) + bias_ref[...].astype(F32))
        top = functools.reduce(jnp.maximum, [jnp.max(x, axis=-1, keepdims=True) for x in scores])
        total = 0.0
        for x, place in zip(scores, places):
            total = total + mm(jnp.exp2(x - top).astype(BF16), val_s[s, place, :])
        results.append(total / total[:, head : head + 1])
    for j in range(peers):
        block = jnp.concatenate([r[j * tokens : (j + 1) * tokens] for r in results], axis=0)
        out_ref[j] = block.T[:head].astype(BF16)


def attend(order, own, far, biases, samples, head):
    sources, _, lanes = own.shape
    tokens = lanes // samples
    width = 128
    peers = 4
    rows = peers * tokens
    total = sources * tokens
    cols = biases[0].shape[1]
    whole = lambda a: pl.BlockSpec(a.shape, lambda i, *_: (0,) * a.ndim)
    return pl.pallas_call(
        attend_kernel,
        grid_spec=pltpu.PrefetchScalarGridSpec(
            num_scalar_prefetch=1,
            grid=(sources // peers,),
            in_specs=[whole(own), whole(far)] + [pl.BlockSpec((rows, cols), lambda i, *_: (i, 0))] * 4,
            out_specs=pl.BlockSpec((peers, head, lanes), lambda i, *_: (i, 0, 0)),
            scratch_shapes=[
                pltpu.VMEM((samples, total, width), BF16),
                pltpu.VMEM((samples, 2 * total, width), BF16),
                pltpu.VMEM((samples, 2 * total, width), BF16),
            ],
        ),
        out_shape=jax.ShapeDtypeStruct((sources, head, lanes), BF16),
        compiler_params=params(),
        cost_estimate=pl.CostEstimate(flops=10**10, bytes_accessed=8 * 10**6, transcendentals=10**7),
        name="attend",
    )(order, own, far, *biases)


def finish_kernel(
    heads_ref, gate_ref, token_in_ref, output_ref, trans_in_ref, trans_out_ref, to_atom_ref, mid_ref, token_ref,
    update_ref, token_out_ref, atom_ref, feature_s,
):
    samples, tokens, channels = token_in_ref.shape
    lanes = samples * tokens
    step = pl.program_id(0)

    @pl.when(step == 0)
    def _():
        attended = heads_ref[...].reshape(channels, lanes).astype(F32).T
        gated = (gate_ref[...] * attended).astype(BF16)
        after = token_in_ref[...].reshape(lanes, channels) + mm(gated, output_ref[...])
        hidden_in = norm_rows(after).astype(BF16)
        hidden_width = trans_out_ref.shape[0]
        left = mm(hidden_in, trans_in_ref[:, :hidden_width])
        right = mm(hidden_in, trans_in_ref[:, hidden_width:])
        hidden = (jax.nn.silu(left) * right).astype(BF16)
        result = (after + mm(hidden, trans_out_ref[...])).astype(BF16)
        token_out_ref[...] = result.reshape(samples, tokens, channels)
        feature_s[...] = mm(result, to_atom_ref[...]).astype(BF16).reshape(feature_s.shape)

    owner = token_ref[...]
    slots = owner.shape[1]
    onehot = (lax.broadcasted_iota(jnp.int32, (tokens, slots), 0) == owner).astype(BF16)
    final = mid_ref[0] + mm(onehot, feature_s[step], TN)
    update = lax.dot_general(
        update_ref[...], norm_rows(final), NT, precision=lax.Precision.HIGHEST, preferred_element_type=F32
    )
    atom_ref[0] = update[:3] * (owner < tokens).astype(F32)


def finish(heads, gate, token_in, tok_output, transition_in, transition_out, token_to_atom, atom_mid, atom_token, pos_update):
    samples, tokens, channels = token_in.shape
    slots, width = atom_mid.shape[1:]
    atom_token = atom_token.reshape(1, slots)
    turned = jnp.pad(pos_update.T, ((0, 5), (0, 0)))
    whole = lambda a: pl.BlockSpec(a.shape, lambda s: (0,) * a.ndim)
    args = (heads, gate, token_in, tok_output, transition_in, transition_out, token_to_atom)
    return pl.pallas_call(
        finish_kernel,
        grid=(samples,),
        in_specs=[whole(a) for a in args]
        + [pl.BlockSpec((1, slots, width), lambda s: (s, 0, 0)), whole(atom_token), whole(turned)],
        out_specs=[
            pl.BlockSpec((samples, tokens, channels), lambda s: (0, 0, 0)),
            pl.BlockSpec((1, 3, slots), lambda s: (s, 0, 0)),
        ],
        out_shape=[
            jax.ShapeDtypeStruct((samples, tokens, channels), BF16),
            jax.ShapeDtypeStruct((samples, 3, slots), F32),
        ],
        scratch_shapes=[pltpu.VMEM((samples, tokens, width), BF16)],
        compiler_params=params(),
        cost_estimate=pl.CostEstimate(flops=3 * 10**9, bytes_accessed=15 * 10**6, transcendentals=10**6),
        name="finish",
    )(*args, atom_mid, atom_token, turned)


def swap(x, axis):
    return lax.ppermute(x, axis, [(0, 1), (1, 0)])


def per_device(
    atom_cond, atom_pos, atom_token, pos_weight, atom_proj, atom_output, atom_to_token, tok_single, ada_weight,
    pair_rep, pair_weight, tok_proj, tok_output, transition_in, transition_out, token_to_atom, pos_update,
):
    tokens, channels = tok_single.shape
    heads = pair_weight.shape[1]
    head = channels // heads
    samples = atom_pos.shape[0]
    bias = pair_bias(pair_rep, pair_weight)
    bias = lax.all_to_all(bias, ("y", "z"), 0, 0, tiled=True)
    bias = bias.reshape(heads * tokens, bias.shape[2])
    across = swap(bias, "xlo")
    bias = (bias, swap(bias, "core"), across, swap(across, "core"))
    atom_mid, token_in = atom_stage(
        atom_cond, atom_pos, atom_token, pos_weight, atom_proj, atom_output, atom_to_token, tokens
    )
    qkv, gate = project(token_in, tok_single, ada_weight, tok_proj, heads)
    own = lax.all_to_all(qkv, ("y", "z"), 0, 0, tiled=True)
    far = swap(own[:, head:], "xhi")
    order = jnp.stack([lax.axis_index("xlo") * 2 + lax.axis_index("core"), lax.axis_index("xhi")]).astype(jnp.int32)
    attended = attend(order, own, far, bias, samples, head)
    attended = lax.all_to_all(attended, ("y", "z"), 0, 0, tiled=True)
    return finish(
        attended, gate, token_in, tok_output, transition_in, transition_out, token_to_atom, atom_mid, atom_token,
        pos_update,
    )


def solution(mesh):
    fine = Mesh(mesh.devices.reshape(2, 2, 2, 4, 4), ("xlo", "core", "xhi", "y", "z"))
    tok = ("xhi", "y", "z")
    sample = ("xlo", "core")
    return jax.shard_map(
        per_device,
        mesh=fine,
        in_specs=(
            P(tok, None), P(sample, None, tok), P(tok), P(), P(), P(), P(), P(tok, None), P(),
            P(tok, sample, None), P(), P(), P(), P(), P(), P(), P(),
        ),
        out_specs=(P(sample, tok, None), P(sample, None, tok)),
        check_vma=False,
    )
```

```python
import functools

import jax
import jax.numpy as jnp
import numpy as np
from jax import lax
from jax.experimental import pallas as pl
from jax.experimental.pallas import tpu as pltpu
from jax.sharding import Mesh, PartitionSpec as P

ATOM_HEADS = 4
QUERY_BLOCK = 32
KEY_WINDOW = 128
NORM_EPSILON = 1e-05
MASKED_SCORE = -1000000000.0
LOG2E = 1.4426950408889634
F32 = jnp.float32
BF16 = jnp.bfloat16
VMEM_LIMIT = 60 * 1024 * 1024

TN = (((0,), (0,)), ((), ()))
NT = (((1,), (1,)), ((), ()))
NN = (((1,), (0,)), ((), ()))


def mm(a, b, dims=NN):
    return lax.dot_general(a, b, dims, preferred_element_type=F32)


def norm_rows(inputs):
    row_mean = jnp.mean(inputs, axis=-1, keepdims=True)
    centered = inputs - row_mean
    variance = jnp.mean(centered * centered, axis=-1, keepdims=True)
    return centered * lax.rsqrt(variance + NORM_EPSILON)


def params():
    return pltpu.CompilerParams(vmem_limit_bytes=VMEM_LIMIT)


def pair_kernel(pair_ref, weight_ref, out_ref, center_s):
    rows, cols, width = pair_ref.shape
    heads = weight_ref.shape[0]

    @pl.when(pl.program_id(0) == 0)
    def _():
        same = lax.broadcasted_iota(jnp.int32, (width, width), 0) == lax.broadcasted_iota(jnp.int32, (width, width), 1)
        center_s[...] = (same.astype(F32) - 1.0 / width).astype(BF16)

    ones = jnp.full((heads, width), 1.0 / width, BF16)
    flat = pair_ref[...].reshape(rows * cols, width)
    centered = mm(flat, center_s[...])
    top = mm(weight_ref[...], centered.astype(BF16), NT)
    variance = mm(ones, (centered * centered).astype(BF16), NT)
    bias = top * (lax.rsqrt(variance + NORM_EPSILON) * LOG2E)
    for h in range(heads):
        block = bias[h : h + 1].reshape(rows, cols).astype(BF16)
        for k in range(out_ref.shape[0]):
            out_ref[k, h] = block


def pair_bias(pair_rep, pair_weight, copies):
    rows, cols, width = pair_rep.shape
    heads = pair_weight.shape[1]
    step = 16
    return pl.pallas_call(
        pair_kernel,
        grid=(rows // step,),
        in_specs=[
            pl.BlockSpec((step, cols, width), lambda i: (i, 0, 0)),
            pl.BlockSpec((heads, width), lambda i: (0, 0)),
        ],
        out_specs=pl.BlockSpec((copies, heads, step, cols), lambda i: (0, 0, i, 0)),
        out_shape=jax.ShapeDtypeStruct((copies, heads, rows, cols), BF16),
        scratch_shapes=[pltpu.VMEM((width, width), BF16)],
        compiler_params=params(),
        cost_estimate=pl.CostEstimate(flops=10**10, bytes_accessed=10**7, transcendentals=0),
        name="pair_bias",
    )(pair_rep, pair_weight.T)


def split_three(value, order):
    first = value.astype(BF16).astype(F32)
    second = (value - first).astype(BF16).astype(F32)
    third = value - first - second
    terms = (first, second, third)
    return [terms[k] for k in order]


def atom_kernel(
    base, cond_ref, pos_ref, token_ref, pos_weight_ref, proj_ref, output_ref, to_token_ref,
    *refs,
):
    mid_ref, token_in_ref, query_s, key_s, val_s, mixed_s, pos_s, weight_s = refs[-8:]
    slots, width = cond_ref.shape
    tokens = token_in_ref.shape[1]
    head = width // ATOM_HEADS
    owner = token_ref[...]
    count = jnp.sum((owner < tokens).astype(jnp.int32))

    @pl.when(pl.program_id(0) == 0)
    def _():
        pos_s[...] = jnp.zeros_like(pos_s)
        weight_s[...] = jnp.zeros_like(weight_s)
        for k, piece in enumerate(split_three(pos_weight_ref[...], (0, 0, 0, 1, 1, 2))):
            weight_s[8 * k : 8 * k + 3, :] = piece
        val_s[:, width:] = jnp.ones((slots, width), BF16)

    position = pos_ref[:, pl.ds(base + pl.program_id(0), 1), :].reshape(3, slots)
    for k, piece in enumerate(split_three(position, (0, 1, 2, 0, 1, 0))):
        pos_s[8 * k : 8 * k + 3, :] = piece
    act = cond_ref[...].astype(F32) + mm(pos_s[...].astype(BF16), weight_s[...].astype(BF16), TN)
    normed = norm_rows(act).astype(BF16)
    projected = mm(normed, proj_ref[...])
    query_s[...] = (projected[:, :width] * (head ** (-0.5) * LOG2E)).astype(BF16)
    key_s[...] = projected[:, width : 2 * width].astype(BF16)
    val_s[:, :width] = projected[:, 2 * width :].astype(BF16)
    stacked = ATOM_HEADS * QUERY_BLOCK
    of_row = lax.broadcasted_iota(jnp.int32, (stacked, width), 0) // QUERY_BLOCK
    of_lane = lax.broadcasted_iota(jnp.int32, (stacked, width), 1) // head
    own_head = of_row == of_lane
    lane = lax.broadcasted_iota(jnp.int32, (stacked, KEY_WINDOW), 1)
    blocks = slots // QUERY_BLOCK
    group = 8
    for first in range(0, blocks, group):
        starts = [
            min(max(b * QUERY_BLOCK - (KEY_WINDOW - QUERY_BLOCK) // 2, 0), slots - KEY_WINDOW)
            for b in range(first, first + group)
        ]
        scores = []
        for k, start in enumerate(starts):
            low = (first + k) * QUERY_BLOCK
            query = query_s[low : low + QUERY_BLOCK, :]
            query = jnp.concatenate([query] * ATOM_HEADS, axis=0)
            query = jnp.where(own_head, query, jnp.zeros_like(query))
            score = mm(query, key_s[start : start + KEY_WINDOW, :], NT)
            scores.append(jnp.where(lane < count - start, score, MASKED_SCORE))
        weights = [jnp.exp2(s - jnp.max(s, axis=-1, keepdims=True)).astype(BF16) for s in scores]
        for k, start in enumerate(starts):
            low = (first + k) * QUERY_BLOCK
            summed = mm(weights[k], val_s[start : start + KEY_WINDOW, :])
            mixed = jnp.where(own_head, summed[:, :width] / summed[:, width:], 0.0)
            mixed = mixed.reshape(ATOM_HEADS, QUERY_BLOCK, width).sum(axis=0)
            mixed_s[low : low + QUERY_BLOCK, :] = mixed.astype(BF16)
    mid = act + mm(mixed_s[...], output_ref[...])
    mid_ref[0] = mid
    feature = jnp.maximum(mm(mid.astype(BF16), to_token_ref[...]), 0.0).astype(BF16)
    onehot = lax.broadcasted_iota(jnp.int32, (tokens, slots), 0) == owner
    members = jnp.sum(onehot.astype(F32), axis=1, keepdims=True)
    token_in_ref[0] = mm(onehot.astype(BF16), feature) / members


def atom_stage(atom_cond, atom_pos, atom_token, pos_weight, atom_proj, atom_output, atom_to_token, tokens, base, samples, all_samples, mid):
    slots, width = atom_cond.shape
    channels = atom_to_token.shape[1]
    whole = lambda a: pl.BlockSpec(a.shape, lambda s: (0,) * a.ndim)
    atom_token = atom_token.reshape(1, slots)
    earlier = () if mid is None else (mid,)
    return pl.pallas_call(
        functools.partial(atom_kernel, base),
        grid=(samples,),
        in_specs=[
            whole(atom_cond),
            whole(atom_pos),
            whole(atom_token),
            whole(pos_weight),
            whole(atom_proj),
            whole(atom_output),
            whole(atom_to_token),
        ] + [pl.BlockSpec(memory_space=pl.ANY)] * len(earlier),
        input_output_aliases={7: 0} if earlier else {},
        out_specs=[
            pl.BlockSpec((1, slots, width), lambda s: (base + s, 0, 0)),
            pl.BlockSpec((1, tokens, channels), lambda s: (s, 0, 0)),
        ],
        out_shape=[
            jax.ShapeDtypeStruct((all_samples, slots, width), F32),
            jax.ShapeDtypeStruct((samples, tokens, channels), F32),
        ],
        scratch_shapes=[
            pltpu.VMEM((slots, width), BF16),
            pltpu.VMEM((slots, width), BF16),
            pltpu.VMEM((slots, 2 * width), BF16),
            pltpu.VMEM((slots, width), BF16),
            pltpu.VMEM((48, slots), F32),
            pltpu.VMEM((48, width), F32),
        ],
        compiler_params=params(),
        cost_estimate=pl.CostEstimate(flops=samples * 6 * 10**9, bytes_accessed=10**6, transcendentals=0),
        name="atom_stage",
    )(atom_cond, atom_pos, atom_token, pos_weight, atom_proj, atom_output, atom_to_token, *earlier)


def project_kernel(token_in_ref, single_ref, ada_ref, proj_ref, *refs):
    heads_ref, gate_ref = refs[-2:]
    samples, tokens, channels = token_in_ref.shape
    copies, heads, _, lanes = heads_ref.shape
    head = channels // heads
    conditioning = 1.0 + mm(single_ref[...], ada_ref[...])
    adapted = (norm_rows(token_in_ref[...]) * conditioning[None]).astype(BF16).reshape(lanes, channels)
    for part in range(3):
        rows = mm(adapted, proj_ref[:, part * channels : (part + 1) * channels])
        if part == 0:
            rows = rows * (head ** (-0.5) * LOG2E)
        turned = rows.T.astype(BF16).reshape(heads, head, lanes)
        for k in range(copies):
            heads_ref[k, :, part * head : (part + 1) * head, :] = turned
    gate = mm(adapted, proj_ref[:, 3 * channels :])
    gate_ref[...] = jax.nn.sigmoid(gate)


def project(token_in, tok_single, ada_weight, tok_proj, heads, copies, half, halves, gate):
    samples, tokens, channels = token_in.shape
    lanes = samples * tokens
    head = channels // heads
    earlier = () if gate is None else (gate,)
    whole = lambda a: pl.BlockSpec(a.shape, lambda i: (0,) * a.ndim)
    args = (token_in, tok_single, ada_weight, tok_proj)
    return pl.pallas_call(
        project_kernel,
        grid=(1,),
        in_specs=[whole(a) for a in args] + [pl.BlockSpec(memory_space=pl.ANY)] * len(earlier),
        out_specs=[
            pl.BlockSpec((copies, heads, 3 * head, lanes), lambda i: (0, 0, 0, 0)),
            pl.BlockSpec((lanes, channels), lambda i: (half, 0)),
        ],
        out_shape=[
            jax.ShapeDtypeStruct((copies, heads, 3 * head, lanes), BF16),
            jax.ShapeDtypeStruct((halves * lanes, channels), F32),
        ],
        input_output_aliases={4: 1} if earlier else {},
        compiler_params=params(),
        cost_estimate=pl.CostEstimate(flops=4 * 10**9, bytes_accessed=8 * 10**6, transcendentals=0),
        name="project",
    )(*args, *earlier)


def attend_kernel(order_ref, heads_ref, near_ref, other_ref, *refs):
    out_ref, query_s, key_s, val_s = refs[-4:]
    peers, head, lanes = out_ref.shape
    samples, _, keys = key_s.shape
    tokens = lanes // samples
    width = val_s.shape[2]
    sources = heads_ref.shape[0]
    cols = near_ref.shape[2]
    step = pl.program_id(0)
    core = order_ref[0]
    first = order_ref[1]

    @pl.when(step == 0)
    def _():
        fill = jnp.zeros((width - head, lanes), F32)
        fill_v = jnp.where(lax.broadcasted_iota(jnp.int32, (width - head, lanes), 0) == 0, 1.0, 0.0)

        def turn(block, below):
            return jnp.concatenate([block.astype(F32), below], axis=0).T.astype(BF16)

        for j in range(sources // 2):
            query = turn(heads_ref[first + j, :head, :], fill)
            for s in range(samples):
                query_s[s, j * tokens : (j + 1) * tokens, :] = query[s * tokens : (s + 1) * tokens, :head]
        for j in range(sources):
            val = turn(heads_ref[j, 2 * head :, :], fill_v)
            for s in range(samples):
                val_s[s, j * tokens : (j + 1) * tokens, :] = val[s * tokens : (s + 1) * tokens]
        for j in range(0, sources, 2):
            for s in range(samples):
                pair = [heads_ref[k, head : 2 * head, s * tokens : (s + 1) * tokens] for k in (j, j + 1)]
                key_s[s, :, j * tokens : (j + 2) * tokens] = jnp.concatenate(pair, axis=1)

    rows = peers * tokens
    results = []
    for s in range(samples):
        query = query_s[s, pl.ds(pl.multiple_of(step * rows, rows), rows), :]
        scores = []
        places = []
        for ref, which in ((near_ref, core), (other_ref, 1 - core)):
            for k in range(2):
                place = pl.ds(pl.multiple_of((2 * k + which) * cols, cols), cols)
                places.append(place)
                scores.append(mm(query, key_s[s, :, place]) + ref[k].astype(F32))
        top = functools.reduce(jnp.maximum, scores)
        top = jnp.max(top, axis=-1, keepdims=True)
        total = 0.0
        for x, place in zip(scores, places):
            total = total + mm(jnp.exp2(x - top).astype(BF16), val_s[s, place, :])
        results.append(total / total[:, head : head + 1])
    for j in range(peers):
        block = jnp.concatenate([r[j * tokens : (j + 1) * tokens] for r in results], axis=0)
        out_ref[j] = block.T[:head].astype(BF16)


def attend(order, qkv, near, other, samples, half, halves, result):
    sources, triple, lanes = qkv.shape
    head = triple // 3
    tokens = lanes // samples
    width = 128
    peers = 4
    rows = peers * tokens
    total = sources * tokens
    cols = near.shape[2]
    earlier = () if result is None else (result,)
    return pl.pallas_call(
        attend_kernel,
        grid_spec=pltpu.PrefetchScalarGridSpec(
            num_scalar_prefetch=1,
            grid=(total // 2 // rows,),
            in_specs=[pl.BlockSpec(qkv.shape, lambda i, *_: (0, 0, 0))]
            + [pl.BlockSpec((2, rows, cols), lambda i, *_: (0, i, 0))] * 2
            + [pl.BlockSpec(memory_space=pl.ANY)] * len(earlier),
            out_specs=pl.BlockSpec((peers, head, lanes), lambda i, *_: (i, half, 0)),
            scratch_shapes=[
                pltpu.VMEM((samples, total // 2, head), BF16),
                pltpu.VMEM((samples, head, total), BF16),
                pltpu.VMEM((samples, total, width), BF16),
            ],
        ),
        out_shape=jax.ShapeDtypeStruct((sources // 2, halves * head, lanes), BF16),
        input_output_aliases={4: 0} if earlier else {},
        compiler_params=params(),
        cost_estimate=pl.CostEstimate(flops=samples * 5 * 10**9, bytes_accessed=10**6, transcendentals=0),
        name="attend",
    )(order, qkv, near, other, *earlier)


def finish_kernel(
    heads_ref, gate_ref, output_ref, trans_in_ref, trans_out_ref, to_atom_ref, mid_ref, owner_ref, update_ref, *refs
):
    token_in_refs, (token_out_ref, atom_ref, feature_s) = refs[:-3], refs[-3:]
    samples, tokens, channels = token_out_ref.shape
    step = pl.program_id(0)

    @pl.when(step == 0)
    def _():
        halves = len(token_in_refs)
        head = heads_ref.shape[1] // halves
        lanes = heads_ref.shape[2]
        attended = [heads_ref[:, k * head : (k + 1) * head, :].reshape(channels, lanes) for k in range(halves)]
        attended = jnp.concatenate([x.astype(F32).T for x in attended], axis=0)
        gated = (gate_ref[...] * attended).astype(BF16)
        token_in = jnp.concatenate([ref[...].reshape(lanes, channels) for ref in token_in_refs], axis=0)
        after = token_in + mm(gated, output_ref[...])
        hidden_in = norm_rows(after).astype(BF16)
        hidden_width = trans_out_ref.shape[0]
        left = mm(hidden_in, trans_in_ref[:, :hidden_width])
        right = mm(hidden_in, trans_in_ref[:, hidden_width:])
        hidden = (jax.nn.silu(left) * right).astype(BF16)
        result = (after + mm(hidden, trans_out_ref[...])).astype(BF16)
        token_out_ref[...] = result.reshape(samples, tokens, channels)
        feature_s[...] = mm(result, to_atom_ref[...]).astype(BF16).reshape(feature_s.shape)

    owner = owner_ref[...]
    slots = owner.shape[1]
    onehot = (lax.broadcasted_iota(jnp.int32, (tokens, slots), 0) == owner).astype(BF16)
    final = norm_rows(mid_ref[0] + mm(onehot, feature_s[step], TN))
    weight = update_ref[...]
    high = final.astype(BF16)
    low = (final - high.astype(F32)).astype(BF16)
    first = weight.astype(BF16)
    second = (weight - first.astype(F32)).astype(BF16)
    update = mm(first, high, NT) + (mm(second, high, NT) + mm(first, low, NT))
    update = update[:3] * (owner < tokens).astype(F32)
    atom_ref[:, pl.ds(step, 1), :] = update.reshape(3, 1, slots)


def finish(
    heads, gate, tok_output, transition_in, transition_out, token_to_atom, atom_mid, atom_token, pos_update, token_in
):
    each, tokens, channels = token_in[0].shape
    samples, slots, width = atom_mid.shape
    owner = atom_token.reshape(1, slots)
    turned = jnp.pad(pos_update.T, ((0, 5), (0, 0)))
    whole = lambda a: pl.BlockSpec(a.shape, lambda s: (0,) * a.ndim)
    args = (heads, gate, tok_output, transition_in, transition_out, token_to_atom)
    return pl.pallas_call(
        finish_kernel,
        grid=(samples,),
        in_specs=[whole(a) for a in args]
        + [pl.BlockSpec((1, slots, width), lambda s: (s, 0, 0)), whole(owner), whole(turned)]
        + [whole(a) for a in token_in],
        out_specs=[
            pl.BlockSpec((samples, tokens, channels), lambda s: (0, 0, 0)),
            pl.BlockSpec((3, samples, slots), lambda s: (0, 0, 0)),
        ],
        out_shape=[
            jax.ShapeDtypeStruct((samples, tokens, channels), BF16),
            jax.ShapeDtypeStruct((3, samples, slots), F32),
        ],
        scratch_shapes=[pltpu.VMEM((samples, tokens, width), BF16)],
        compiler_params=params(),
        cost_estimate=pl.CostEstimate(flops=8 * 10**9, bytes_accessed=10**7, transcendentals=0),
        name="finish",
    )(*args, atom_mid, owner, turned, *token_in)


def exchange(x, axes):
    return lax.all_to_all(x, axes, 0, 0, tiled=True)


def per_device(
    atom_cond, atom_pos, atom_token, pos_weight, atom_proj, atom_output, atom_to_token, tok_single, ada_weight,
    pair_rep, pair_weight, tok_proj, tok_output, transition_in, transition_out, token_to_atom, pos_update,
):
    tokens, channels = tok_single.shape
    heads = pair_weight.shape[1]
    samples = atom_pos.shape[0]
    halves = 2
    each = samples // halves
    pos = jnp.swapaxes(atom_pos, 0, 1)
    order = jnp.stack([lax.axis_index("core"), lax.axis_index("xhi") * heads]).astype(jnp.int32)
    bias = pair_bias(pair_rep, pair_weight, 2)
    near = exchange(bias.reshape((2 * heads,) + bias.shape[2:]), ("xlo", "y", "z"))
    near = near.reshape(2, heads * tokens, near.shape[2])
    other = lax.ppermute(near, "core", [(0, 1), (1, 0)])
    inputs, received = [], []
    mid = gate = None
    for k in range(halves):
        mid, token_in = atom_stage(
            atom_cond, pos, atom_token, pos_weight, atom_proj, atom_output, atom_to_token, tokens, k * each, each,
            samples, mid,
        )
        qkv, gate = project(token_in, tok_single, ada_weight, tok_proj, heads, 2, k, halves, gate)
        inputs.append(token_in)
        received.append(exchange(qkv.reshape((2 * heads,) + qkv.shape[2:]), ("xhi", "y", "z")))
    attended = None
    for k in range(halves):
        attended = attend(order, received[k], near, other, each, k, halves, attended)
    attended = exchange(attended, ("y", "z"))
    token_out, update = finish(
        attended, gate, tok_output, transition_in, transition_out, token_to_atom, mid, atom_token, pos_update, inputs
    )
    return token_out, jnp.swapaxes(update, 0, 1)


def solution(mesh):
    fine = Mesh(mesh.devices.reshape(2, 2, 2, 4, 4), ("xlo", "core", "xhi", "y", "z"))
    tok = ("xhi", "y", "z")
    sample = ("xlo", "core")
    return jax.shard_map(
        per_device,
        mesh=fine,
        in_specs=(
            P(tok, None), P(sample, None, tok), P(tok), P(), P(), P(), P(), P(tok, None), P(),
            P(tok, sample, None), P(), P(), P(), P(), P(), P(), P(),
        ),
        out_specs=(P(sample, tok, None), P(sample, None, tok)),
        check_vma=False,
    )
```

```python
import functools

import jax
import jax.numpy as jnp
import numpy as np
from jax import lax
from jax.experimental import pallas as pl
from jax.experimental.pallas import tpu as pltpu
from jax.sharding import Mesh, PartitionSpec as P

ATOM_HEADS = 4
QUERY_BLOCK = 32
KEY_WINDOW = 128
NORM_EPSILON = 1e-05
MASKED_SCORE = -1000000000.0
LOG2E = 1.4426950408889634
F32 = jnp.float32
BF16 = jnp.bfloat16
VMEM_LIMIT = 60 * 1024 * 1024

TN = (((0,), (0,)), ((), ()))
NT = (((1,), (1,)), ((), ()))
NN = (((1,), (0,)), ((), ()))


def flat_row(ref):
    return jnp.concatenate([ref[i : i + 1, :] for i in range(ref.shape[0])], axis=1)


def mm(a, b, dims=NN):
    return lax.dot_general(a, b, dims, preferred_element_type=F32)


def norm_rows(inputs):
    row_mean = jnp.mean(inputs, axis=-1, keepdims=True)
    centered = inputs - row_mean
    variance = jnp.mean(centered * centered, axis=-1, keepdims=True)
    return centered * lax.rsqrt(variance + NORM_EPSILON)


def params():
    return pltpu.CompilerParams(vmem_limit_bytes=VMEM_LIMIT)


def pair_kernel(pair_ref, weight_ref, out_ref, center_s):
    rows, cols, width = pair_ref.shape
    heads = weight_ref.shape[0]

    @pl.when(pl.program_id(0) == 0)
    def _():
        same = lax.broadcasted_iota(jnp.int32, (width, width), 0) == lax.broadcasted_iota(jnp.int32, (width, width), 1)
        center_s[...] = (same.astype(F32) - 1.0 / width).astype(BF16)

    flat = pair_ref[...].reshape(rows * cols, width)
    centered = mm(center_s[...], flat, NT)
    variance = jnp.mean(centered * centered, axis=0, keepdims=True)
    top = mm(weight_ref[...], centered.astype(BF16))
    bias = top * (lax.rsqrt(variance + NORM_EPSILON) * LOG2E)
    for h in range(heads):
        out_ref[h] = bias[h : h + 1].reshape(rows, cols).astype(BF16)


def pair_bias(pair_rep, pair_weight):
    rows, cols, width = pair_rep.shape
    heads = pair_weight.shape[1]
    step = 16
    return pl.pallas_call(
        pair_kernel,
        grid=(rows // step,),
        in_specs=[
            pl.BlockSpec((step, cols, width), lambda i: (i, 0, 0)),
            pl.BlockSpec((heads, width), lambda i: (0, 0)),
        ],
        out_specs=pl.BlockSpec((heads, step, cols), lambda i: (0, i, 0)),
        out_shape=jax.ShapeDtypeStruct((heads, rows, cols), BF16),
        scratch_shapes=[pltpu.VMEM((width, width), BF16)],
        compiler_params=params(),
        cost_estimate=pl.CostEstimate(flops=10**10, bytes_accessed=10**7, transcendentals=0),
        name="pair_bias",
    )(pair_rep, pair_weight.T)


def split_three(value, order):
    first = value.astype(BF16).astype(F32)
    second = (value - first).astype(BF16).astype(F32)
    third = value - first - second
    terms = (first, second, third)
    return [terms[k] for k in order]


def atom_kernel(
    base, cond_ref, pos_ref, token_ref, pos_weight_ref, proj_ref, output_ref, to_token_ref,
    *refs,
):
    mid_ref, token_in_ref, query_s, key_s, val_s, mixed_s, pos_s, weight_s = refs[-8:]
    slots, width = cond_ref.shape
    tokens = token_in_ref.shape[1]
    head = width // ATOM_HEADS
    owner = flat_row(token_ref)
    count = jnp.sum((owner < tokens).astype(jnp.int32))

    @pl.when(pl.program_id(0) == 0)
    def _():
        pos_s[...] = jnp.zeros_like(pos_s)
        weight_s[...] = jnp.zeros_like(weight_s)
        for k, piece in enumerate(split_three(pos_weight_ref[...], (0, 0, 0, 1, 1, 2))):
            weight_s[8 * k : 8 * k + 3, :] = piece
        val_s[:, width:] = jnp.ones((slots, width), BF16)

    position = pos_ref[:, pl.ds(base + pl.program_id(0), 1), :].reshape(3, slots)
    for k, piece in enumerate(split_three(position, (0, 1, 2, 0, 1, 0))):
        pos_s[8 * k : 8 * k + 3, :] = piece
    act = cond_ref[...].astype(F32) + mm(pos_s[...].astype(BF16), weight_s[...].astype(BF16), TN)
    normed = norm_rows(act).astype(BF16)
    projected = mm(normed, proj_ref[...])
    query_s[...] = (projected[:, :width] * (head ** (-0.5) * LOG2E)).astype(BF16)
    key_s[...] = projected[:, width : 2 * width].astype(BF16)
    val_s[:, :width] = projected[:, 2 * width :].astype(BF16)
    stacked = ATOM_HEADS * QUERY_BLOCK
    of_row = lax.broadcasted_iota(jnp.int32, (stacked, width), 0) // QUERY_BLOCK
    of_lane = lax.broadcasted_iota(jnp.int32, (stacked, width), 1) // head
    own_head = of_row == of_lane
    lane = lax.broadcasted_iota(jnp.int32, (stacked, KEY_WINDOW), 1)
    blocks = slots // QUERY_BLOCK
    group = 16
    for first in range(0, blocks, group):
        starts = [
            min(max(b * QUERY_BLOCK - (KEY_WINDOW - QUERY_BLOCK) // 2, 0), slots - KEY_WINDOW)
            for b in range(first, first + group)
        ]
        scores = []
        for k, start in enumerate(starts):
            low = (first + k) * QUERY_BLOCK
            query = query_s[low : low + QUERY_BLOCK, :]
            query = jnp.concatenate([query] * ATOM_HEADS, axis=0)
            query = jnp.where(own_head, query, jnp.zeros_like(query))
            score = mm(query, key_s[start : start + KEY_WINDOW, :], NT)
            scores.append(jnp.where(lane < count - start, score, MASKED_SCORE))
        weights = [jnp.exp2(s - jnp.max(s, axis=-1, keepdims=True)).astype(BF16) for s in scores]
        for k, start in enumerate(starts):
            low = (first + k) * QUERY_BLOCK
            summed = mm(weights[k], val_s[start : start + KEY_WINDOW, :])
            mixed = jnp.where(own_head, summed[:, :width] / summed[:, width:], 0.0)
            mixed = mixed.reshape(ATOM_HEADS, QUERY_BLOCK, width).sum(axis=0)
            mixed_s[low : low + QUERY_BLOCK, :] = mixed.astype(BF16)
    mid = act + mm(mixed_s[...], output_ref[...])
    mid_ref[0] = mid
    feature = jnp.maximum(mm(mid.astype(BF16), to_token_ref[...]), 0.0).astype(BF16)
    onehot = lax.broadcasted_iota(jnp.int32, (tokens, slots), 0) == owner
    members = jnp.sum(onehot.astype(F32), axis=1, keepdims=True)
    token_in_ref[0] = mm(onehot.astype(BF16), feature) / members


def atom_stage(atom_cond, atom_pos, atom_token, pos_weight, atom_proj, atom_output, atom_to_token, tokens, base, samples, all_samples, mid):
    slots, width = atom_cond.shape
    channels = atom_to_token.shape[1]
    whole = lambda a: pl.BlockSpec(a.shape, lambda s: (0,) * a.ndim)
    atom_token = atom_token.reshape(slots // width, width)
    earlier = () if mid is None else (mid,)
    return pl.pallas_call(
        functools.partial(atom_kernel, base),
        grid=(samples,),
        in_specs=[
            whole(atom_cond),
            whole(atom_pos),
            whole(atom_token),
            whole(pos_weight),
            whole(atom_proj),
            whole(atom_output),
            whole(atom_to_token),
        ] + [pl.BlockSpec(memory_space=pl.ANY)] * len(earlier),
        input_output_aliases={7: 0} if earlier else {},
        out_specs=[
            pl.BlockSpec((1, slots, width), lambda s: (base + s, 0, 0)),
            pl.BlockSpec((1, tokens, channels), lambda s: (s, 0, 0)),
        ],
        out_shape=[
            jax.ShapeDtypeStruct((all_samples, slots, width), F32),
            jax.ShapeDtypeStruct((samples, tokens, channels), F32),
        ],
        scratch_shapes=[
            pltpu.VMEM((slots, width), BF16),
            pltpu.VMEM((slots, width), BF16),
            pltpu.VMEM((slots, 2 * width), BF16),
            pltpu.VMEM((slots, width), BF16),
            pltpu.VMEM((48, slots), F32),
            pltpu.VMEM((48, width), F32),
        ],
        compiler_params=params(),
        cost_estimate=pl.CostEstimate(flops=samples * 6 * 10**9, bytes_accessed=10**6, transcendentals=0),
        name="atom_stage",
    )(atom_cond, atom_pos, atom_token, pos_weight, atom_proj, atom_output, atom_to_token, *earlier)


def project_kernel(*refs):
    token_in_refs, (single_ref, ada_ref, proj_ref, heads_ref, gate_ref) = refs[:-5], refs[-5:]
    channels = proj_ref.shape[0]
    heads, triple, lanes = heads_ref.shape
    head = triple // 3
    conditioning = 1.0 + mm(single_ref[...], ada_ref[...])
    adapted = [(norm_rows(ref[...]) * conditioning[None]).astype(BF16).reshape(-1, channels) for ref in token_in_refs]
    adapted = jnp.concatenate(adapted, axis=0)
    for part in range(3):
        rows = mm(adapted, proj_ref[:, part * channels : (part + 1) * channels])
        if part == 0:
            rows = rows * (head ** (-0.5) * LOG2E)
        heads_ref[:, part * head : (part + 1) * head, :] = rows.T.astype(BF16).reshape(heads, head, lanes)
    gate_ref[...] = jax.nn.sigmoid(mm(adapted, proj_ref[:, 3 * channels :]))


def project(token_in, tok_single, ada_weight, tok_proj, heads):
    tokens, channels = tok_single.shape
    lanes = sum(x.shape[0] for x in token_in) * tokens
    head = channels // heads
    return pl.pallas_call(
        project_kernel,
        out_shape=[
            jax.ShapeDtypeStruct((heads, 3 * head, lanes), BF16),
            jax.ShapeDtypeStruct((lanes, channels), F32),
        ],
        compiler_params=params(),
        cost_estimate=pl.CostEstimate(flops=4 * 10**9, bytes_accessed=8 * 10**6, transcendentals=0),
        name="project",
    )(*token_in, tok_single, ada_weight, tok_proj)


def attend_kernel(last, order_ref, own_ref, *refs):
    refs, (out_ref, query_s, key_s, val_s) = refs[:-4], refs[-4:]
    heads_ref, refs = (refs[0], refs[1:]) if last else (own_ref, refs)
    bias_refs, earlier = refs[:4], refs[4:]
    sources, _, lanes = own_ref.shape
    samples, head, keys = key_s.shape
    tokens = lanes // samples
    width = val_s.shape[2]
    rows, cols = bias_refs[0].shape
    step = pl.program_id(0)
    mine = order_ref[0]
    half = 1 - order_ref[1] if last else order_ref[1]

    @pl.when(step == 0)
    def _():
        fill = jnp.zeros((width - head, lanes), F32)
        fill_v = jnp.where(lax.broadcasted_iota(jnp.int32, (width - head, lanes), 0) == 0, 1.0, 0.0)

        def turn(block, below):
            return jnp.concatenate([block.astype(F32), below], axis=0).T.astype(BF16)

        low = 0 if last else head
        for j in range(sources):
            query = turn(own_ref[j, :head, :], fill)
            val = turn(heads_ref[j, low + head :, :], fill_v)
            for s in range(samples):
                query_s[s, j * tokens : (j + 1) * tokens, :] = query[s * tokens : (s + 1) * tokens, :head]
                val_s[s, j * tokens : (j + 1) * tokens, :] = val[s * tokens : (s + 1) * tokens]
        for j in range(0, sources, 2):
            for s in range(samples):
                pair = [heads_ref[k, low : low + head, s * tokens : (s + 1) * tokens] for k in (j, j + 1)]
                key_s[s, :, j * tokens : (j + 2) * tokens] = jnp.concatenate(pair, axis=1)

    swapped = mine // 2 != half
    biases = [jnp.where(swapped, bias_refs[p + 2][...], bias_refs[p][...]).astype(F32) for p in range(2)]
    places = [pl.ds(pl.multiple_of((mine % 2 ^ p) * cols, cols), cols) for p in range(2)]
    lane = lax.broadcasted_iota(jnp.int32, (256, width), 1)
    results = []
    unit = 256
    jobs = [(r, s) for r in range(0, rows, unit) for s in range(samples)]

    def score(job):
        r, s = job
        query = query_s[s, pl.ds(pl.multiple_of(step * rows + r, unit), unit), :]
        return [mm(query, key_s[s, :, place]) + bias[r : r + unit] for place, bias in zip(places, biases)]

    def soften(job, scores):
        r, s = job
        top = jnp.max(jnp.maximum(*scores), axis=-1, keepdims=True)
        total = 0.0
        if last:
            before = earlier[0][s, r : r + unit]
            top_before = before[:, width - 1 :]
            top = jnp.maximum(top, top_before)
            total = before * jnp.exp2(top_before - top)
        return job, top, total, [jnp.exp2(x - top).astype(BF16) for x in scores]

    def gather(state):
        (r, s), top, total, weights = state
        for x, place in zip(weights, places):
            total = total + mm(x, val_s[s, place, :])
        if last:
            results.append(total / total[:, head : head + 1])
        else:
            out_ref[s, r : r + unit] = jnp.where(lane == width - 1, top, total)

    ahead, state = score(jobs[0]), None
    for n, job in enumerate(jobs):
        scores = ahead
        if n + 1 < len(jobs):
            ahead = score(jobs[n + 1])
        if state is not None:
            gather(state)
        state = soften(job, scores)
    gather(state)
    if last:
        for j in range(rows // tokens):
            u, low = j * tokens // unit * samples, j * tokens % unit
            block = jnp.concatenate([r[low : low + tokens] for r in results[u : u + samples]], axis=0)
            out_ref[j] = block.T[:head].astype(BF16)


def attend(order, own, biases, samples, far=None, earlier=None):
    sources, triple, lanes = own.shape
    head = triple // 3
    tokens = lanes // samples
    width = 128
    rows = 256
    total, cols = biases[0].shape
    last = earlier is not None
    whole = lambda a: pl.BlockSpec(a.shape, lambda i, *_: (0,) * a.ndim)
    bias_specs = [pl.BlockSpec((rows, cols), lambda i, *_: (i, 0))] * 4
    running = pl.BlockSpec((samples, rows, width), lambda i, *_: (0, i, 0))
    if last:
        args, in_specs = (own, far, *biases, earlier), [whole(own), whole(far)] + bias_specs + [running]
        out_specs = pl.BlockSpec((rows // tokens, head, lanes), lambda i, *_: (i, 0, 0))
        out_shape = jax.ShapeDtypeStruct((sources, head, lanes), BF16)
    else:
        args, in_specs = (own, *biases), [whole(own)] + bias_specs
        out_specs = running
        out_shape = jax.ShapeDtypeStruct((samples, total, width), F32)
    return pl.pallas_call(
        functools.partial(attend_kernel, last),
        grid_spec=pltpu.PrefetchScalarGridSpec(
            num_scalar_prefetch=1,
            grid=(total // rows,),
            in_specs=in_specs,
            out_specs=out_specs,
            scratch_shapes=[
                pltpu.VMEM((samples, total, head), BF16),
                pltpu.VMEM((samples, head, total), BF16),
                pltpu.VMEM((samples, total, width), BF16),
            ],
        ),
        out_shape=out_shape,
        compiler_params=params(),
        cost_estimate=pl.CostEstimate(flops=10**10, bytes_accessed=10**6, transcendentals=0),
        name="attend",
    )(order, *args)


def finish_kernel(
    heads_ref, gate_ref, output_ref, to_atom_ref, mid_ref, owner_ref, update_ref, trans_in_hbm, trans_out_hbm, *refs
):
    token_in_refs, (token_out_ref, atom_ref, feature_s, trans_in_ref, trans_out_ref, sems) = refs[:-6], refs[-6:]
    samples, tokens, channels = token_out_ref.shape
    step = pl.program_id(0)

    @pl.when(step == 0)
    def _():
        load_in = pltpu.make_async_copy(trans_in_hbm, trans_in_ref, sems.at[0])
        load_out = pltpu.make_async_copy(trans_out_hbm, trans_out_ref, sems.at[1])
        load_in.start()
        load_out.start()
        lanes = heads_ref.shape[2]
        attended = heads_ref[...].reshape(channels, lanes).astype(F32).T
        gated = (gate_ref[...] * attended).astype(BF16)
        token_in = jnp.concatenate([ref[...].reshape(-1, channels) for ref in token_in_refs], axis=0)
        after = token_in + mm(gated, output_ref[...])
        hidden_in = norm_rows(after).astype(BF16)
        hidden_width = trans_out_ref.shape[0]
        load_in.wait()
        left = mm(hidden_in, trans_in_ref[:, :hidden_width])
        right = mm(hidden_in, trans_in_ref[:, hidden_width:])
        hidden = (jax.nn.silu(left) * right).astype(BF16)
        load_out.wait()
        result = (after + mm(hidden, trans_out_ref[...])).astype(BF16)
        token_out_ref[...] = result.reshape(samples, tokens, channels)
        feature_s[...] = mm(result, to_atom_ref[...]).astype(BF16).reshape(feature_s.shape)

    owner = flat_row(owner_ref)
    slots = owner.shape[1]
    onehot = (lax.broadcasted_iota(jnp.int32, (tokens, slots), 0) == owner).astype(BF16)
    final = norm_rows(mid_ref[0] + mm(onehot, feature_s[step], TN))
    weight = update_ref[...]
    high = final.astype(BF16)
    low = (final - high.astype(F32)).astype(BF16)
    first = weight.astype(BF16)
    second = (weight - first.astype(F32)).astype(BF16)
    update = mm(first, high, NT) + (mm(second, high, NT) + mm(first, low, NT))
    update = update * (owner < tokens).astype(F32)
    atom_ref[:, pl.ds(step, 1), :] = update.reshape(3, 1, slots)


def finish(
    heads, gate, tok_output, transition_in, transition_out, token_to_atom, atom_mid, atom_token, pos_update, token_in
):
    each, tokens, channels = token_in[0].shape
    samples, slots, width = atom_mid.shape
    owner = atom_token.reshape(slots // width, width)
    turned = pos_update.T
    whole = lambda a: pl.BlockSpec(a.shape, lambda s: (0,) * a.ndim)
    args = (heads, gate, tok_output, token_to_atom)
    return pl.pallas_call(
        finish_kernel,
        grid=(samples,),
        in_specs=[whole(a) for a in args]
        + [pl.BlockSpec((1, slots, width), lambda s: (s, 0, 0)), whole(owner), whole(turned)]
        + [pl.BlockSpec(memory_space=pl.ANY)] * 2
        + [whole(a) for a in token_in],
        out_specs=[
            pl.BlockSpec((samples, tokens, channels), lambda s: (0, 0, 0)),
            pl.BlockSpec((3, samples, slots), lambda s: (0, 0, 0)),
        ],
        out_shape=[
            jax.ShapeDtypeStruct((samples, tokens, channels), BF16),
            jax.ShapeDtypeStruct((3, samples, slots), F32),
        ],
        scratch_shapes=[
            pltpu.VMEM((samples, tokens, width), BF16),
            pltpu.VMEM(transition_in.shape, BF16),
            pltpu.VMEM(transition_out.shape, BF16),
            pltpu.SemaphoreType.DMA((2,)),
        ],
        compiler_params=params(),
        cost_estimate=pl.CostEstimate(flops=8 * 10**9, bytes_accessed=10**7, transcendentals=0),
        name="finish",
    )(*args, atom_mid, owner, turned, transition_in, transition_out, *token_in)


def swap(x, axis):
    return lax.ppermute(x, axis, [(0, 1), (1, 0)])


def exchange(x, axes):
    return lax.all_to_all(x, axes, 0, 0, tiled=True)


def per_device(
    atom_cond, atom_pos, atom_token, pos_weight, atom_proj, atom_output, atom_to_token, tok_single, ada_weight,
    pair_rep, pair_weight, tok_proj, tok_output, transition_in, transition_out, token_to_atom, pos_update,
):
    tokens, channels = tok_single.shape
    heads = pair_weight.shape[1]
    samples = atom_pos.shape[0]
    halves = 2
    each = samples // halves
    pos = jnp.swapaxes(atom_pos, 0, 1)
    order = jnp.stack([lax.axis_index("xlo") * 2 + lax.axis_index("core"), lax.axis_index("xhi")]).astype(jnp.int32)
    own_bias = exchange(pair_bias(pair_rep, pair_weight), ("y", "z"))
    own_bias = own_bias.reshape(heads * tokens, own_bias.shape[2])
    inputs = []
    mid = None
    for k in range(halves):
        mid, token_in = atom_stage(
            atom_cond, pos, atom_token, pos_weight, atom_proj, atom_output, atom_to_token, tokens, k * each, each,
            samples, mid,
        )
        inputs.append(token_in)
    own_bias, inputs[1] = lax.optimization_barrier((own_bias, inputs[1]))
    across = swap(own_bias, "xlo")
    near = swap(own_bias, "core")
    qkv, gate = project(inputs, tok_single, ada_weight, tok_proj, heads)
    own = exchange(qkv, ("y", "z"))
    far = swap(own[:, channels // heads :], "xhi")
    biases = (own_bias, near, across, swap(across, "core"))
    running = attend(order, own, biases, samples)
    attended = attend(order, own, biases, samples, far, running)
    attended = exchange(attended, ("y", "z"))
    token_out, update = finish(
        attended, gate, tok_output, transition_in, transition_out, token_to_atom, mid, atom_token, pos_update, inputs
    )
    return token_out, jnp.swapaxes(update, 0, 1)


def solution(mesh):
    fine = Mesh(mesh.devices.reshape(2, 2, 2, 4, 4), ("xlo", "core", "xhi", "y", "z"))
    tok = ("xhi", "y", "z")
    sample = ("xlo", "core")
    return jax.shard_map(
        per_device,
        mesh=fine,
        in_specs=(
            P(tok, None), P(sample, None, tok), P(tok), P(), P(), P(), P(), P(tok, None), P(),
            P(tok, sample, None), P(), P(), P(), P(), P(), P(), P(),
        ),
        out_specs=(P(sample, tok, None), P(sample, None, tok)),
        check_vma=False,
    )
```

```python
import functools

import jax
import jax.numpy as jnp
import numpy as np
from jax import lax
from jax.experimental import pallas as pl
from jax.experimental.pallas import tpu as pltpu
from jax.sharding import Mesh, PartitionSpec as P

ATOM_HEADS = 4
QUERY_BLOCK = 32
KEY_WINDOW = 128
NORM_EPSILON = 1e-05
MASKED_SCORE = -1000000000.0
LOG2E = 1.4426950408889634
F32 = jnp.float32
BF16 = jnp.bfloat16
VMEM_LIMIT = 117 * 512 * 1024
PAIR_VMEM_LIMIT = 60 * 1024 * 1024
ATTEND_VMEM_LIMIT = 44 * 1024 * 1024
FINISH_VMEM_LIMIT = 52 * 1024 * 1024

TN = (((0,), (0,)), ((), ()))
NT = (((1,), (1,)), ((), ()))
NN = (((1,), (0,)), ((), ()))


def flat_row(ref):
    return jnp.concatenate([ref[i : i + 1, :] for i in range(ref.shape[0])], axis=1)


def mm(a, b, dims=NN):
    return lax.dot_general(a, b, dims, preferred_element_type=F32)


def norm_rows(inputs):
    row_mean = jnp.mean(inputs, axis=-1, keepdims=True)
    centered = inputs - row_mean
    variance = jnp.mean(centered * centered, axis=-1, keepdims=True)
    return centered * lax.rsqrt(variance + NORM_EPSILON)


def params(limit=VMEM_LIMIT):
    return pltpu.CompilerParams(vmem_limit_bytes=limit)


def pair_kernel(pair_ref, weight_ref, out_ref, center_s):
    rows, cols, width = pair_ref.shape
    heads = weight_ref.shape[0]

    @pl.when(pl.program_id(0) == 0)
    def _():
        same = lax.broadcasted_iota(jnp.int32, (width, width), 0) == lax.broadcasted_iota(jnp.int32, (width, width), 1)
        center_s[...] = (same.astype(F32) - 1.0 / width).astype(BF16)

    flat = pair_ref[...].reshape(rows * cols, width)
    centered = mm(center_s[...], flat, NT)
    variance = jnp.mean(centered * centered, axis=0, keepdims=True)
    top = mm(weight_ref[...], centered.astype(BF16))
    bias = top * (lax.rsqrt(variance + NORM_EPSILON) * LOG2E)
    for h in range(heads):
        out_ref[h] = bias[h : h + 1].reshape(rows, cols).astype(BF16)


def pair_bias(pair_rep, pair_weight):
    rows, cols, width = pair_rep.shape
    heads = pair_weight.shape[1]
    step = 32
    return pl.pallas_call(
        pair_kernel,
        grid=(rows // step,),
        in_specs=[
            pl.BlockSpec((step, cols, width), lambda i: (i, 0, 0)),
            pl.BlockSpec((heads, width), lambda i: (0, 0)),
        ],
        out_specs=pl.BlockSpec((heads, step, cols), lambda i: (0, i, 0)),
        out_shape=jax.ShapeDtypeStruct((heads, rows, cols), BF16),
        scratch_shapes=[pltpu.VMEM((width, width), BF16)],
        compiler_params=params(PAIR_VMEM_LIMIT),
        cost_estimate=pl.CostEstimate(flops=10**10, bytes_accessed=10**7, transcendentals=0),
        name="pair_bias",
    )(pair_rep, pair_weight.T)


def split_three(value, order):
    first = value.astype(BF16).astype(F32)
    second = (value - first).astype(BF16).astype(F32)
    third = value - first - second
    terms = (first, second, third)
    return [terms[k] for k in order]


def atom_kernel(
    cond_ref, pos_ref, token_ref, pos_weight_ref, proj_ref, output_ref, to_token_ref, single_ref, ada_hbm, tok_proj_hbm,
    mid_ref, token_in_ref, heads_ref, adapted_ref,
    query_s, key_s, val_s, mixed_s, pos_s, weight_s, token_s, ada_ref, tok_proj_ref, sems,
):
    slots, width = cond_ref.shape
    tokens, channels = token_in_ref.shape[1:]
    heads, triple, lanes = heads_ref.shape
    sample = pl.program_id(0)
    load_ada = pltpu.make_async_copy(ada_hbm, ada_ref, sems.at[0])
    load_proj = pltpu.make_async_copy(tok_proj_hbm.at[:, pl.ds(0, 3 * channels)], tok_proj_ref, sems.at[1])
    head = width // ATOM_HEADS
    owner = flat_row(token_ref)
    count = jnp.sum((owner < tokens).astype(jnp.int32))

    @pl.when(sample == 0)
    def _():
        load_ada.start()
        load_proj.start()
        pos_s[...] = jnp.zeros_like(pos_s)
        weight_s[...] = jnp.zeros_like(weight_s)
        for k, piece in enumerate(split_three(pos_weight_ref[...], (0, 0, 0, 1, 1, 2))):
            weight_s[8 * k : 8 * k + 3, :] = piece
        val_s[:, width:] = jnp.ones((slots, width), BF16)

    position = pos_ref[:, pl.ds(sample, 1), :].reshape(3, slots)
    for k, piece in enumerate(split_three(position, (0, 1, 2, 0, 1, 0))):
        pos_s[8 * k : 8 * k + 3, :] = piece
    act = cond_ref[...].astype(F32) + mm(pos_s[...].astype(BF16), weight_s[...].astype(BF16), TN)
    normed = norm_rows(act).astype(BF16)
    projected = mm(normed, proj_ref[...])
    query_s[...] = (projected[:, :width] * (head ** (-0.5) * LOG2E)).astype(BF16)
    key_s[...] = projected[:, width : 2 * width].astype(BF16)
    val_s[:, :width] = projected[:, 2 * width :].astype(BF16)
    stacked = ATOM_HEADS * QUERY_BLOCK
    of_row = lax.broadcasted_iota(jnp.int32, (stacked, width), 0) // QUERY_BLOCK
    of_lane = lax.broadcasted_iota(jnp.int32, (stacked, width), 1) // head
    own_head = of_row == of_lane
    lane = lax.broadcasted_iota(jnp.int32, (stacked, KEY_WINDOW), 1)
    blocks = slots // QUERY_BLOCK
    group = 16
    for first in range(0, blocks, group):
        starts = [
            min(max(b * QUERY_BLOCK - (KEY_WINDOW - QUERY_BLOCK) // 2, 0), slots - KEY_WINDOW)
            for b in range(first, first + group)
        ]
        scores = []
        for k, start in enumerate(starts):
            low = (first + k) * QUERY_BLOCK
            query = query_s[low : low + QUERY_BLOCK, :]
            query = jnp.concatenate([query] * ATOM_HEADS, axis=0)
            query = jnp.where(own_head, query, jnp.zeros_like(query))
            score = mm(query, key_s[start : start + KEY_WINDOW, :], NT)
            scores.append(jnp.where(lane < count - start, score, MASKED_SCORE))
        weights = [jnp.exp2(s - jnp.max(s, axis=-1, keepdims=True)).astype(BF16) for s in scores]
        for k, start in enumerate(starts):
            low = (first + k) * QUERY_BLOCK
            summed = mm(weights[k], val_s[start : start + KEY_WINDOW, :])
            mixed = jnp.where(own_head, summed[:, :width] / summed[:, width:], 0.0)
            mixed = mixed.reshape(ATOM_HEADS, QUERY_BLOCK, width).sum(axis=0)
            mixed_s[low : low + QUERY_BLOCK, :] = mixed.astype(BF16)
    mid = act + mm(mixed_s[...], output_ref[...])
    mid_ref[0] = mid
    feature = jnp.maximum(mm(mid.astype(BF16), to_token_ref[...]), 0.0).astype(BF16)
    onehot = lax.broadcasted_iota(jnp.int32, (tokens, slots), 0) == owner
    members = jnp.sum(onehot.astype(F32), axis=1, keepdims=True)
    token_in = mm(onehot.astype(BF16), feature) / members
    token_in_ref[0] = token_in
    token_s[pl.ds(pl.multiple_of(sample * tokens, tokens), tokens), :] = norm_rows(token_in)

    @pl.when(sample == pl.num_programs(0) - 1)
    def _():
        load_ada.wait()
        load_proj.wait()
        conditioning = 1.0 + mm(single_ref[...], ada_ref[...])
        normed_tokens = token_s[...].reshape(lanes // tokens, tokens, channels)
        adapted = (normed_tokens * conditioning[None]).astype(BF16).reshape(lanes, channels)
        adapted_ref[...] = adapted
        size = triple // 3
        for part in range(3):
            rows = mm(adapted, tok_proj_ref[:, part * channels : (part + 1) * channels])
            if part == 0:
                rows = rows * (size ** (-0.5) * LOG2E)
            heads_ref[:, part * size : (part + 1) * size, :] = rows.T.astype(BF16).reshape(heads, size, lanes)


def atom_stage(
    atom_cond, atom_pos, atom_token, pos_weight, atom_proj, atom_output, atom_to_token, tok_single, ada_weight, tok_proj, heads
):
    samples = atom_pos.shape[1]
    slots, width = atom_cond.shape
    tokens, channels = tok_single.shape
    lanes = samples * tokens
    triple = 3 * channels // heads
    whole = lambda a: pl.BlockSpec(a.shape, lambda s: (0,) * a.ndim)
    atom_token = atom_token.reshape(slots // width, width)
    args = (atom_cond, atom_pos, atom_token, pos_weight, atom_proj, atom_output, atom_to_token, tok_single)
    return pl.pallas_call(
        atom_kernel,
        grid=(samples,),
        in_specs=[whole(a) for a in args] + [pl.BlockSpec(memory_space=pl.ANY)] * 2,
        out_specs=[
            pl.BlockSpec((1, slots, width), lambda s: (s, 0, 0)),
            pl.BlockSpec((1, tokens, channels), lambda s: (s, 0, 0)),
            pl.BlockSpec((heads, triple, lanes), lambda s: (0, 0, 0)),
            pl.BlockSpec((lanes, channels), lambda s: (0, 0)),
        ],
        out_shape=[
            jax.ShapeDtypeStruct((samples, slots, width), F32),
            jax.ShapeDtypeStruct((samples, tokens, channels), F32),
            jax.ShapeDtypeStruct((heads, triple, lanes), BF16),
            jax.ShapeDtypeStruct((lanes, channels), BF16),
        ],
        scratch_shapes=[
            pltpu.VMEM((slots, width), BF16),
            pltpu.VMEM((slots, width), BF16),
            pltpu.VMEM((slots, 2 * width), BF16),
            pltpu.VMEM((slots, width), BF16),
            pltpu.VMEM((48, slots), F32),
            pltpu.VMEM((48, width), F32),
            pltpu.VMEM((lanes, channels), F32),
            pltpu.VMEM((channels, channels), BF16),
            pltpu.VMEM((channels, 3 * channels), BF16),
            pltpu.SemaphoreType.DMA((2,)),
        ],
        compiler_params=params(),
        cost_estimate=pl.CostEstimate(flops=20 * 10**9, bytes_accessed=10**7, transcendentals=0),
        name="atom_stage",
    )(*args, ada_weight, tok_proj)


def gate_kernel(adapted_ref, proj_ref, update_ref, gate_ref, terms_ref):
    gate_ref[...] = jax.nn.sigmoid(mm(adapted_ref[...], proj_ref[...]))
    weight = update_ref[...]
    first = weight.astype(BF16).astype(F32)
    terms_ref[...] = jnp.zeros_like(terms_ref)
    terms_ref[0:3, :] = first
    terms_ref[8:11, :] = weight - first


def project_gate(adapted, tok_proj, pos_update):
    lanes, channels = adapted.shape
    turned = pos_update.T
    return pl.pallas_call(
        gate_kernel,
        grid=(1,),
        in_specs=[
            pl.BlockSpec((lanes, channels), lambda i: (0, 0)),
            pl.BlockSpec((channels, channels), lambda i: (0, 3)),
            pl.BlockSpec(turned.shape, lambda i: (0, 0)),
        ],
        out_specs=[
            pl.BlockSpec((lanes, channels), lambda i: (0, 0)),
            pl.BlockSpec((16, turned.shape[1]), lambda i: (0, 0)),
        ],
        out_shape=[
            jax.ShapeDtypeStruct((lanes, channels), F32),
            jax.ShapeDtypeStruct((16, turned.shape[1]), F32),
        ],
        compiler_params=params(),
        cost_estimate=pl.CostEstimate(flops=10**9, bytes_accessed=2 * 10**6, transcendentals=0),
        name="project_gate",
    )(adapted, tok_proj, turned)


def attend_kernel(last, order_ref, own_ref, *refs):
    refs, (out_ref, query_s, key_s, val_s) = refs[:-4], refs[-4:]
    heads_ref, refs = (refs[0], refs[1:]) if last else (own_ref, refs)
    bias_refs, earlier = refs[:4], refs[4:]
    sources, _, lanes = own_ref.shape
    samples, head, keys = key_s.shape
    tokens = lanes // samples
    width = val_s.shape[2]
    rows, cols = bias_refs[0].shape
    step = pl.program_id(0)
    mine = order_ref[0]
    half = 1 - order_ref[1] if last else order_ref[1]

    @pl.when(step == 0)
    def _():
        fill = jnp.zeros((width - head, lanes), F32)
        fill_v = jnp.where(lax.broadcasted_iota(jnp.int32, (width - head, lanes), 0) == 0, 1.0, 0.0)

        def turn(block, below):
            return jnp.concatenate([block.astype(F32), below], axis=0).T.astype(BF16)

        low = 0 if last else head
        for j in range(sources):
            query = turn(own_ref[j, :head, :], fill)
            val = turn(heads_ref[j, low + head :, :], fill_v)
            for s in range(samples):
                query_s[s, j * tokens : (j + 1) * tokens, :] = query[s * tokens : (s + 1) * tokens, :head]
                val_s[s, j * tokens : (j + 1) * tokens, :] = val[s * tokens : (s + 1) * tokens]
        for j in range(0, sources, 2):
            for s in range(samples):
                pair = [heads_ref[k, low : low + head, s * tokens : (s + 1) * tokens] for k in (j, j + 1)]
                key_s[s, :, j * tokens : (j + 2) * tokens] = jnp.concatenate(pair, axis=1)

    swapped = mine // 2 != half
    biases = [jnp.where(swapped, bias_refs[p + 2][...], bias_refs[p][...]).astype(F32) for p in range(2)]
    places = [pl.ds(pl.multiple_of((mine % 2 ^ p) * cols, cols), cols) for p in range(2)]
    lane = lax.broadcasted_iota(jnp.int32, (256, width), 1)
    results = []
    unit = 256
    jobs = [(r, s) for r in range(0, rows, unit) for s in range(samples)]

    def score(job):
        r, s = job
        query = query_s[s, pl.ds(pl.multiple_of(step * rows + r, unit), unit), :]
        return [mm(query, key_s[s, :, place]) + bias[r : r + unit] for place, bias in zip(places, biases)]

    def soften(job, scores):
        r, s = job
        top = jnp.max(jnp.maximum(*scores), axis=-1, keepdims=True)
        total = 0.0
        if last:
            before = earlier[0][s, r : r + unit]
            top_before = before[:, width - 1 :]
            top = jnp.maximum(top, top_before)
            total = before * jnp.exp2(top_before - top)
        return job, top, total, [jnp.exp2(x - top).astype(BF16) for x in scores]

    def gather(state):
        (r, s), top, total, weights = state
        for x, place in zip(weights, places):
            total = total + mm(x, val_s[s, place, :])
        if last:
            results.append(total / total[:, head : head + 1])
        else:
            out_ref[s, r : r + unit] = jnp.where(lane == width - 1, top, total)

    ahead, state = score(jobs[0]), None
    for n, job in enumerate(jobs):
        scores = ahead
        if n + 1 < len(jobs):
            ahead = score(jobs[n + 1])
        if state is not None:
            gather(state)
        state = soften(job, scores)
    gather(state)
    if last:
        for j in range(rows // tokens):
            u, low = j * tokens // unit * samples, j * tokens % unit
            block = jnp.concatenate([r[low : low + tokens] for r in results[u : u + samples]], axis=0)
            out_ref[j] = block.T[:head].astype(BF16)


def attend(order, own, biases, samples, far=None, earlier=None):
    sources, triple, lanes = own.shape
    head = triple // 3
    tokens = lanes // samples
    width = 128
    rows = 256
    total, cols = biases[0].shape
    last = earlier is not None
    whole = lambda a: pl.BlockSpec(a.shape, lambda i, *_: (0,) * a.ndim)
    bias_specs = [pl.BlockSpec((rows, cols), lambda i, *_: (i, 0))] * 4
    running = pl.BlockSpec((samples, rows, width), lambda i, *_: (0, i, 0))
    if last:
        args, in_specs = (own, far, *biases, earlier), [whole(own), whole(far)] + bias_specs + [running]
        out_specs = pl.BlockSpec((rows // tokens, head, lanes), lambda i, *_: (i, 0, 0))
        out_shape = jax.ShapeDtypeStruct((sources, head, lanes), BF16)
    else:
        args, in_specs = (own, *biases), [whole(own)] + bias_specs
        out_specs = running
        out_shape = jax.ShapeDtypeStruct((samples, total, width), F32)
    return pl.pallas_call(
        functools.partial(attend_kernel, last),
        grid_spec=pltpu.PrefetchScalarGridSpec(
            num_scalar_prefetch=1,
            grid=(total // rows,),
            in_specs=in_specs,
            out_specs=out_specs,
            scratch_shapes=[
                pltpu.VMEM((samples, total, head), BF16),
                pltpu.VMEM((samples, head, total), BF16),
                pltpu.VMEM((samples, total, width), BF16),
            ],
        ),
        out_shape=out_shape,
        compiler_params=params(ATTEND_VMEM_LIMIT),
        cost_estimate=pl.CostEstimate(flops=10**10, bytes_accessed=10**6, transcendentals=0),
        name="attend",
    )(order, *args)


def finish_kernel(
    heads_ref, gate_ref, output_ref, to_atom_ref, mid_ref, owner_ref, update_ref, trans_in_hbm, trans_out_hbm, *refs
):
    token_in_refs, (token_out_ref, atom_ref, feature_s, trans_in_ref, trans_out_ref, sems) = refs[:-6], refs[-6:]
    samples, tokens, channels = token_out_ref.shape
    step = pl.program_id(0)

    @pl.when(step == 0)
    def _():
        hidden_width = trans_out_ref.shape[0]
        chunk = hidden_width // 3
        loads = []
        for k in range(3):
            for n, low in enumerate((k * chunk, hidden_width + k * chunk)):
                place = pl.ds(low, chunk)
                loads.append(pltpu.make_async_copy(trans_in_hbm.at[:, place], trans_in_ref.at[:, place], sems.at[2 * k + n]))
        loads.append(pltpu.make_async_copy(trans_out_hbm, trans_out_ref, sems.at[6]))
        for load in loads:
            load.start()
        lanes = heads_ref.shape[2]
        attended = heads_ref[...].reshape(channels, lanes).astype(F32).T
        gated = (gate_ref[...] * attended).astype(BF16)
        token_in = jnp.concatenate([ref[...].reshape(-1, channels) for ref in token_in_refs], axis=0)
        after = token_in + mm(gated, output_ref[...])
        hidden_in = norm_rows(after).astype(BF16)
        hidden = []
        for k in range(3):
            low = k * chunk
            loads[2 * k].wait()
            left = mm(hidden_in, trans_in_ref[:, low : low + chunk])
            loads[2 * k + 1].wait()
            right = mm(hidden_in, trans_in_ref[:, hidden_width + low : hidden_width + low + chunk])
            hidden.append((jax.nn.silu(left) * right).astype(BF16))
        hidden = jnp.concatenate(hidden, axis=1)
        loads[6].wait()
        result = (after + mm(hidden, trans_out_ref[...])).astype(BF16)
        token_out_ref[...] = result.reshape(samples, tokens, channels)
        feature_s[...] = mm(result, to_atom_ref[...]).astype(BF16).reshape(feature_s.shape)

    owner = flat_row(owner_ref)
    slots = owner.shape[1]
    onehot = (lax.broadcasted_iota(jnp.int32, (tokens, slots), 0) == owner).astype(BF16)
    final = norm_rows(mid_ref[0] + mm(onehot, feature_s[step], TN))
    high = final.astype(BF16)
    low = (final - high.astype(F32)).astype(BF16)
    terms = update_ref[...].astype(BF16)
    update = mm(terms, high, NT)
    update = update[:3] + (update[8:11] + mm(terms, low, NT)[:3])
    update = update * (owner < tokens).astype(F32)
    atom_ref[:, pl.ds(step, 1), :] = update.reshape(3, 1, slots)


def finish(
    heads, gate, tok_output, transition_in, transition_out, token_to_atom, atom_mid, atom_token, pos_update, token_in
):
    each, tokens, channels = token_in[0].shape
    samples, slots, width = atom_mid.shape
    owner = atom_token.reshape(slots // width, width)
    turned = pos_update
    whole = lambda a: pl.BlockSpec(a.shape, lambda s: (0,) * a.ndim)
    args = (heads, gate, tok_output, token_to_atom)
    return pl.pallas_call(
        finish_kernel,
        grid=(samples,),
        in_specs=[whole(a) for a in args]
        + [pl.BlockSpec((1, slots, width), lambda s: (s, 0, 0)), whole(owner), whole(turned)]
        + [pl.BlockSpec(memory_space=pl.ANY)] * 2
        + [whole(a) for a in token_in],
        out_specs=[
            pl.BlockSpec((samples, tokens, channels), lambda s: (0, 0, 0)),
            pl.BlockSpec((3, samples, slots), lambda s: (0, 0, 0)),
        ],
        out_shape=[
            jax.ShapeDtypeStruct((samples, tokens, channels), BF16),
            jax.ShapeDtypeStruct((3, samples, slots), F32),
        ],
        scratch_shapes=[
            pltpu.VMEM((samples, tokens, width), BF16),
            pltpu.VMEM(transition_in.shape, BF16),
            pltpu.VMEM(transition_out.shape, BF16),
            pltpu.SemaphoreType.DMA((7,)),
        ],
        compiler_params=params(FINISH_VMEM_LIMIT),
        cost_estimate=pl.CostEstimate(flops=8 * 10**9, bytes_accessed=10**7, transcendentals=0),
        name="finish",
    )(*args, atom_mid, owner, turned, transition_in, transition_out, *token_in)


def swap(x, axis):
    return lax.ppermute(x, axis, [(0, 1), (1, 0)])


def exchange(x, axes):
    return lax.all_to_all(x, axes, 0, 0, tiled=True)


def per_device(
    atom_cond, atom_pos, atom_token, pos_weight, atom_proj, atom_output, atom_to_token, tok_single, ada_weight,
    pair_rep, pair_weight, tok_proj, tok_output, transition_in, transition_out, token_to_atom, pos_update,
):
    tokens, channels = tok_single.shape
    heads = pair_weight.shape[1]
    samples = atom_pos.shape[0]
    pos = jnp.swapaxes(atom_pos, 0, 1)
    order = jnp.stack([lax.axis_index("xlo") * 2 + lax.axis_index("core"), lax.axis_index("xhi")]).astype(jnp.int32)
    own_bias = exchange(pair_bias(pair_rep, pair_weight), ("y", "z"))
    own_bias = own_bias.reshape(heads * tokens, own_bias.shape[2])
    mid, token_in, qkv, adapted = atom_stage(
        atom_cond, pos, atom_token, pos_weight, atom_proj, atom_output, atom_to_token, tok_single, ada_weight, tok_proj,
        heads,
    )
    own_bias, qkv = lax.optimization_barrier((own_bias, qkv))
    across = swap(own_bias, "xlo")
    near = swap(own_bias, "core")
    own = exchange(qkv, ("y", "z"))
    gate, terms = project_gate(adapted, tok_proj, pos_update)
    across, gate = lax.optimization_barrier((across, gate))
    far = swap(own[:, channels // heads :], "xhi")
    biases = (own_bias, near, across, swap(across, "core"))
    running = attend(order, own, biases, samples)
    attended = attend(order, own, biases, samples, far, running)
    attended = exchange(attended, ("y", "z"))
    token_out, update = finish(
        attended, gate, tok_output, transition_in, transition_out, token_to_atom, mid, atom_token, terms, [token_in]
    )
    return token_out, jnp.swapaxes(update, 0, 1)


def solution(mesh):
    fine = Mesh(mesh.devices.reshape(2, 2, 2, 4, 4), ("xlo", "core", "xhi", "y", "z"))
    tok = ("xhi", "y", "z")
    sample = ("xlo", "core")
    return jax.shard_map(
        per_device,
        mesh=fine,
        in_specs=(
            P(tok, None), P(sample, None, tok), P(tok), P(), P(), P(), P(), P(tok, None), P(),
            P(tok, sample, None), P(), P(), P(), P(), P(), P(), P(),
        ),
        out_specs=(P(sample, tok, None), P(sample, None, tok)),
        check_vma=False,
    )
```

```python
import functools

import jax
import jax.numpy as jnp
import numpy as np
from jax import lax
from jax.experimental import pallas as pl
from jax.experimental.pallas import tpu as pltpu
from jax.sharding import Mesh, PartitionSpec as P

ATOM_HEADS = 4
QUERY_BLOCK = 32
KEY_WINDOW = 128
NORM_EPSILON = 1e-05
MASKED_SCORE = -1000000000.0
LOG2E = 1.4426950408889634
F32 = jnp.float32
BF16 = jnp.bfloat16
VMEM_LIMIT = 117 * 512 * 1024
PAIR_VMEM_LIMIT = 60 * 1024 * 1024
ATTEND_VMEM_LIMIT = 44 * 1024 * 1024
FINISH_VMEM_LIMIT = 52 * 1024 * 1024

TN = (((0,), (0,)), ((), ()))
NT = (((1,), (1,)), ((), ()))
NN = (((1,), (0,)), ((), ()))


def flat_row(ref):
    return jnp.concatenate([ref[i : i + 1, :] for i in range(ref.shape[0])], axis=1)


def mm(a, b, dims=NN):
    return lax.dot_general(a, b, dims, preferred_element_type=F32)


def norm_rows(inputs):
    row_mean = jnp.mean(inputs, axis=-1, keepdims=True)
    centered = inputs - row_mean
    variance = jnp.mean(centered * centered, axis=-1, keepdims=True)
    return centered * lax.rsqrt(variance + NORM_EPSILON)


def params(limit=VMEM_LIMIT):
    return pltpu.CompilerParams(vmem_limit_bytes=limit)


def pair_kernel(pair_ref, weight_ref, out_ref, center_s):
    rows, cols, width = pair_ref.shape
    heads = weight_ref.shape[0]

    @pl.when(pl.program_id(0) == 0)
    def _():
        same = lax.broadcasted_iota(jnp.int32, (width, width), 0) == lax.broadcasted_iota(jnp.int32, (width, width), 1)
        center_s[...] = (same.astype(F32) - 1.0 / width).astype(BF16)

    flat = pair_ref[...].reshape(rows * cols, width)
    centered = mm(center_s[...], flat, NT)
    variance = jnp.mean(centered * centered, axis=0, keepdims=True)
    top = mm(weight_ref[...], centered.astype(BF16))
    bias = top * (lax.rsqrt(variance + NORM_EPSILON) * LOG2E)
    for h in range(heads):
        out_ref[h] = bias[h : h + 1].reshape(rows, cols).astype(BF16)


def pair_bias(pair_rep, pair_weight):
    rows, cols, width = pair_rep.shape
    heads = pair_weight.shape[1]
    step = 32
    return pl.pallas_call(
        pair_kernel,
        grid=(rows // step,),
        in_specs=[
            pl.BlockSpec((step, cols, width), lambda i: (i, 0, 0)),
            pl.BlockSpec((heads, width), lambda i: (0, 0)),
        ],
        out_specs=pl.BlockSpec((heads, step, cols), lambda i: (0, i, 0)),
        out_shape=jax.ShapeDtypeStruct((heads, rows, cols), BF16),
        scratch_shapes=[pltpu.VMEM((width, width), BF16)],
        compiler_params=params(PAIR_VMEM_LIMIT),
        cost_estimate=pl.CostEstimate(flops=10**10, bytes_accessed=10**7, transcendentals=0),
        name="pair_bias",
    )(pair_rep, pair_weight.T)


def split_three(value, order):
    first = value.astype(BF16).astype(F32)
    second = (value - first).astype(BF16).astype(F32)
    third = value - first - second
    terms = (first, second, third)
    return [terms[k] for k in order]


def atom_kernel(
    cond_ref, pos_ref, token_ref, pos_weight_ref, proj_ref, output_ref, to_token_ref, single_ref, ada_hbm, tok_proj_hbm,
    mid_ref, token_in_ref, heads_ref, adapted_ref,
    query_s, key_s, val_s, mixed_s, pos_s, weight_s, token_s, ada_ref, tok_proj_ref, sems,
):
    slots, width = cond_ref.shape
    tokens, channels = token_in_ref.shape[1:]
    heads, triple, lanes = heads_ref.shape
    sample = pl.program_id(0)
    load_ada = pltpu.make_async_copy(ada_hbm, ada_ref, sems.at[0])
    load_proj = pltpu.make_async_copy(tok_proj_hbm.at[:, pl.ds(0, 3 * channels)], tok_proj_ref, sems.at[1])
    head = width // ATOM_HEADS
    owner = flat_row(token_ref)
    count = jnp.sum((owner < tokens).astype(jnp.int32))

    @pl.when(sample == 0)
    def _():
        load_ada.start()
        load_proj.start()
        pos_s[...] = jnp.zeros_like(pos_s)
        weight_s[...] = jnp.zeros_like(weight_s)
        for k, piece in enumerate(split_three(pos_weight_ref[...], (0, 0, 0, 1, 1, 2))):
            weight_s[8 * k : 8 * k + 3, :] = piece
        val_s[:, width:] = jnp.ones((slots, width), BF16)

    position = pos_ref[:, pl.ds(sample, 1), :].reshape(3, slots)
    for k, piece in enumerate(split_three(position, (0, 1, 2, 0, 1, 0))):
        pos_s[8 * k : 8 * k + 3, :] = piece
    act = cond_ref[...].astype(F32) + mm(pos_s[...].astype(BF16), weight_s[...].astype(BF16), TN)
    normed = norm_rows(act).astype(BF16)
    projected = mm(normed, proj_ref[...])
    query_s[...] = (projected[:, :width] * (head ** (-0.5) * LOG2E)).astype(BF16)
    key_s[...] = projected[:, width : 2 * width].astype(BF16)
    val_s[:, :width] = projected[:, 2 * width :].astype(BF16)
    stacked = ATOM_HEADS * QUERY_BLOCK
    of_row = lax.broadcasted_iota(jnp.int32, (stacked, width), 0) // QUERY_BLOCK
    of_lane = lax.broadcasted_iota(jnp.int32, (stacked, width), 1) // head
    own_head = of_row == of_lane
    lane = lax.broadcasted_iota(jnp.int32, (stacked, KEY_WINDOW), 1)
    blocks = slots // QUERY_BLOCK
    group = 16
    for first in range(0, blocks, group):
        starts = [
            min(max(b * QUERY_BLOCK - (KEY_WINDOW - QUERY_BLOCK) // 2, 0), slots - KEY_WINDOW)
            for b in range(first, first + group)
        ]
        scores = []
        for k, start in enumerate(starts):
            low = (first + k) * QUERY_BLOCK
            query = query_s[low : low + QUERY_BLOCK, :]
            query = jnp.concatenate([query] * ATOM_HEADS, axis=0)
            query = jnp.where(own_head, query, jnp.zeros_like(query))
            score = mm(query, key_s[start : start + KEY_WINDOW, :], NT)
            scores.append(jnp.where(lane < count - start, score, MASKED_SCORE))
        weights = [jnp.exp2(s - jnp.max(s, axis=-1, keepdims=True)).astype(BF16) for s in scores]
        for k, start in enumerate(starts):
            low = (first + k) * QUERY_BLOCK
            summed = mm(weights[k], val_s[start : start + KEY_WINDOW, :])
            mixed = jnp.where(own_head, summed[:, :width] / summed[:, width:], 0.0)
            mixed = mixed.reshape(ATOM_HEADS, QUERY_BLOCK, width).sum(axis=0)
            mixed_s[low : low + QUERY_BLOCK, :] = mixed.astype(BF16)
    mid = act + mm(mixed_s[...], output_ref[...])
    mid_ref[0] = mid
    feature = jnp.maximum(mm(mid.astype(BF16), to_token_ref[...]), 0.0).astype(BF16)
    onehot = lax.broadcasted_iota(jnp.int32, (tokens, slots), 0) == owner
    members = jnp.sum(onehot.astype(F32), axis=1, keepdims=True)
    token_in = mm(onehot.astype(BF16), feature) / members
    token_in_ref[0] = token_in
    token_s[pl.ds(pl.multiple_of(sample * tokens, tokens), tokens), :] = norm_rows(token_in)

    @pl.when(sample == pl.num_programs(0) - 1)
    def _():
        load_ada.wait()
        load_proj.wait()
        conditioning = 1.0 + mm(single_ref[...], ada_ref[...])
        normed_tokens = token_s[...].reshape(lanes // tokens, tokens, channels)
        adapted = (normed_tokens * conditioning[None]).astype(BF16).reshape(lanes, channels)
        adapted_ref[...] = adapted
        size = triple // 3
        for part in range(3):
            rows = mm(adapted, tok_proj_ref[:, part * channels : (part + 1) * channels])
            if part == 0:
                rows = rows * (size ** (-0.5) * LOG2E)
            heads_ref[:, part * size : (part + 1) * size, :] = rows.T.astype(BF16).reshape(heads, size, lanes)


def atom_stage(
    atom_cond, atom_pos, atom_token, pos_weight, atom_proj, atom_output, atom_to_token, tok_single, ada_weight, tok_proj, heads
):
    samples = atom_pos.shape[1]
    slots, width = atom_cond.shape
    tokens, channels = tok_single.shape
    lanes = samples * tokens
    triple = 3 * channels // heads
    whole = lambda a: pl.BlockSpec(a.shape, lambda s: (0,) * a.ndim)
    atom_token = atom_token.reshape(slots // width, width)
    args = (atom_cond, atom_pos, atom_token, pos_weight, atom_proj, atom_output, atom_to_token, tok_single)
    return pl.pallas_call(
        atom_kernel,
        grid=(samples,),
        in_specs=[whole(a) for a in args] + [pl.BlockSpec(memory_space=pl.ANY)] * 2,
        out_specs=[
            pl.BlockSpec((1, slots, width), lambda s: (s, 0, 0)),
            pl.BlockSpec((1, tokens, channels), lambda s: (s, 0, 0)),
            pl.BlockSpec((heads, triple, lanes), lambda s: (0, 0, 0)),
            pl.BlockSpec((lanes, channels), lambda s: (0, 0)),
        ],
        out_shape=[
            jax.ShapeDtypeStruct((samples, slots, width), F32),
            jax.ShapeDtypeStruct((samples, tokens, channels), F32),
            jax.ShapeDtypeStruct((heads, triple, lanes), BF16),
            jax.ShapeDtypeStruct((lanes, channels), BF16),
        ],
        scratch_shapes=[
            pltpu.VMEM((slots, width), BF16),
            pltpu.VMEM((slots, width), BF16),
            pltpu.VMEM((slots, 2 * width), BF16),
            pltpu.VMEM((slots, width), BF16),
            pltpu.VMEM((48, slots), F32),
            pltpu.VMEM((48, width), F32),
            pltpu.VMEM((lanes, channels), F32),
            pltpu.VMEM((channels, channels), BF16),
            pltpu.VMEM((channels, 3 * channels), BF16),
            pltpu.SemaphoreType.DMA((2,)),
        ],
        compiler_params=params(),
        cost_estimate=pl.CostEstimate(flops=20 * 10**9, bytes_accessed=10**7, transcendentals=0),
        name="atom_stage",
    )(*args, ada_weight, tok_proj)


def gate_kernel(adapted_ref, proj_ref, update_ref, gate_ref, terms_ref):
    gate_ref[...] = jax.nn.sigmoid(mm(adapted_ref[...], proj_ref[...]))
    weight = update_ref[...]
    first = weight.astype(BF16).astype(F32)
    terms_ref[...] = jnp.zeros_like(terms_ref)
    terms_ref[0:3, :] = first
    terms_ref[8:11, :] = weight - first


def project_gate(adapted, tok_proj, pos_update):
    lanes, channels = adapted.shape
    turned = pos_update.T
    return pl.pallas_call(
        gate_kernel,
        grid=(1,),
        in_specs=[
            pl.BlockSpec((lanes, channels), lambda i: (0, 0)),
            pl.BlockSpec((channels, channels), lambda i: (0, 3)),
            pl.BlockSpec(turned.shape, lambda i: (0, 0)),
        ],
        out_specs=[
            pl.BlockSpec((lanes, channels), lambda i: (0, 0)),
            pl.BlockSpec((16, turned.shape[1]), lambda i: (0, 0)),
        ],
        out_shape=[
            jax.ShapeDtypeStruct((lanes, channels), F32),
            jax.ShapeDtypeStruct((16, turned.shape[1]), F32),
        ],
        compiler_params=params(),
        cost_estimate=pl.CostEstimate(flops=10**9, bytes_accessed=2 * 10**6, transcendentals=0),
        name="project_gate",
    )(adapted, tok_proj, turned)


def attend_kernel(last, order_ref, own_ref, *refs):
    refs, (out_ref, query_s, key_s, val_s, bias_s, sems) = refs[:-6], refs[-6:]
    heads_ref, refs = (refs[0], refs[1:]) if last else (own_ref, refs)
    bias_refs, earlier = refs[:4], refs[4:]
    sources, _, lanes = own_ref.shape
    samples, head, keys = key_s.shape
    tokens = lanes // samples
    width = val_s.shape[2]
    rows = out_ref.shape[0] * tokens if last else out_ref.shape[1]
    cols = bias_s.shape[2]
    unit = 256
    step = pl.program_id(0)
    mine = order_ref[0]
    half = 1 - order_ref[1] if last else order_ref[1]

    swapped = mine // 2 != half

    def load(p, n, other):
        place = pl.ds(pl.multiple_of(n * unit, unit), unit)
        return pltpu.make_async_copy(bias_refs[p + 2 * other].at[place], bias_s.at[p, place], sems.at[p, n])

    @pl.when((step == 0) & swapped)
    def _():
        for n in range(sources * tokens // unit):
            for p in range(2):
                load(p, n, 1).start()

    @pl.when((step == 0) & jnp.logical_not(swapped))
    def _():
        for n in range(sources * tokens // unit):
            for p in range(2):
                load(p, n, 0).start()

    @pl.when(step == 0)
    def _():
        fill = jnp.zeros((width - head, lanes), F32)
        fill_v = jnp.where(lax.broadcasted_iota(jnp.int32, (width - head, lanes), 0) == 0, 1.0, 0.0)

        def turn(block, below):
            return jnp.concatenate([block.astype(F32), below], axis=0).T.astype(BF16)

        low = 0 if last else head
        for j in range(sources):
            query = turn(own_ref[j, :head, :], fill)
            val = turn(heads_ref[j, low + head :, :], fill_v)
            for s in range(samples):
                query_s[s, j * tokens : (j + 1) * tokens, :] = query[s * tokens : (s + 1) * tokens, :head]
                val_s[s, j * tokens : (j + 1) * tokens, :] = val[s * tokens : (s + 1) * tokens]
        for j in range(0, sources, 2):
            for s in range(samples):
                pair = [heads_ref[k, low : low + head, s * tokens : (s + 1) * tokens] for k in (j, j + 1)]
                key_s[s, :, j * tokens : (j + 2) * tokens] = jnp.concatenate(pair, axis=1)

    places = [pl.ds(pl.multiple_of((mine % 2 ^ p) * cols, cols), cols) for p in range(2)]
    lane = lax.broadcasted_iota(jnp.int32, (256, width), 1)
    results = []
    jobs = [(r, s) for r in range(0, rows, unit) for s in range(samples)]

    def score(job):
        r, s = job
        query = query_s[s, pl.ds(pl.multiple_of(step * rows + r, unit), unit), :]
        block = step * (rows // unit) + r // unit
        if s == 0:
            for p in range(2):
                load(p, block, 0).wait()
        block = pl.ds(pl.multiple_of(block * unit, unit), unit)
        return [mm(query, key_s[s, :, place]) + bias_s[p, block, :].astype(F32) for p, place in enumerate(places)]

    def soften(job, scores):
        r, s = job
        top = jnp.max(jnp.maximum(*scores), axis=-1, keepdims=True)
        total = 0.0
        if last:
            before = earlier[0][s, r : r + unit]
            top_before = before[:, width - 1 :]
            top = jnp.maximum(top, top_before)
            total = before * jnp.exp2(top_before - top)
        return job, top, total, [jnp.exp2(x - top).astype(BF16) for x in scores]

    def gather(state):
        (r, s), top, total, weights = state
        for x, place in zip(weights, places):
            total = total + mm(x, val_s[s, place, :])
        if last:
            results.append(total / total[:, head : head + 1])
        else:
            out_ref[s, r : r + unit] = jnp.where(lane == width - 1, top, total)

    ahead, state = score(jobs[0]), None
    for n, job in enumerate(jobs):
        scores = ahead
        if n + 1 < len(jobs):
            ahead = score(jobs[n + 1])
        if state is not None:
            gather(state)
        state = soften(job, scores)
    gather(state)
    if last:
        for j in range(rows // tokens):
            u, low = j * tokens // unit * samples, j * tokens % unit
            block = jnp.concatenate([r[low : low + tokens] for r in results[u : u + samples]], axis=0)
            out_ref[j] = block.T[:head].astype(BF16)


def attend(order, own, biases, samples, far=None, earlier=None, part=0, result=None):
    sources, triple, lanes = own.shape
    head = triple // 3
    tokens = lanes // samples
    width = 128
    total, cols = biases[0].shape
    last = earlier is not None
    rows = 512 if last else 256
    each = far.shape[2] // tokens if last else samples
    spans = each * tokens
    before = () if result is None else (result,)
    own_spec = pl.BlockSpec((sources, triple, spans), lambda i, *_: (0, 0, part))
    bias_specs = [pl.BlockSpec(memory_space=pl.ANY)] * 4
    running = pl.BlockSpec((each, rows, width), lambda i, *_: (part, i, 0))
    if last:
        args = (own, far, *biases, earlier, *before)
        in_specs = [own_spec, pl.BlockSpec(far.shape, lambda i, *_: (0, 0, 0))] + bias_specs + [running]
        in_specs += [pl.BlockSpec(memory_space=pl.ANY)] * len(before)
        out_specs = pl.BlockSpec((rows // tokens, head, spans), lambda i, *_: (i, 0, part))
        out_shape = jax.ShapeDtypeStruct((sources, head, lanes), BF16)
    else:
        args, in_specs = (own, *biases), [own_spec] + bias_specs
        out_specs = running
        out_shape = jax.ShapeDtypeStruct((samples, total, width), F32)
    return pl.pallas_call(
        functools.partial(attend_kernel, last),
        grid_spec=pltpu.PrefetchScalarGridSpec(
            num_scalar_prefetch=1,
            grid=(total // rows,),
            in_specs=in_specs,
            out_specs=out_specs,
            scratch_shapes=[
                pltpu.VMEM((each, total, head), BF16),
                pltpu.VMEM((each, head, total), BF16),
                pltpu.VMEM((each, total, width), BF16),
                pltpu.VMEM((2, total, cols), BF16),
                pltpu.SemaphoreType.DMA((2, total // 256)),
            ],
        ),
        out_shape=out_shape,
        input_output_aliases={8: 0} if before else {},
        compiler_params=params(ATTEND_VMEM_LIMIT),
        cost_estimate=pl.CostEstimate(flops=each * 25 * 10**8, bytes_accessed=10**6, transcendentals=0),
        name="attend",
    )(order, *args)


def finish_kernel(
    heads_ref, gate_ref, output_ref, to_atom_ref, mid_ref, owner_ref, update_ref, trans_in_hbm, trans_out_hbm, *refs
):
    token_in_refs, (token_out_ref, atom_ref, feature_s, trans_in_ref, trans_out_ref, sems) = refs[:-6], refs[-6:]
    samples, tokens, channels = token_out_ref.shape
    step = pl.program_id(0)

    @pl.when(step == 0)
    def _():
        hidden_width = trans_out_ref.shape[0]
        chunk = hidden_width // 3
        loads = []
        for k in range(3):
            for n, low in enumerate((k * chunk, hidden_width + k * chunk)):
                place = pl.ds(low, chunk)
                loads.append(pltpu.make_async_copy(trans_in_hbm.at[:, place], trans_in_ref.at[:, place], sems.at[2 * k + n]))
        loads.append(pltpu.make_async_copy(trans_out_hbm, trans_out_ref, sems.at[6]))
        for load in loads:
            load.start()
        lanes = heads_ref.shape[2]
        attended = heads_ref[...].reshape(channels, lanes).astype(F32).T
        gated = (gate_ref[...] * attended).astype(BF16)
        token_in = jnp.concatenate([ref[...].reshape(-1, channels) for ref in token_in_refs], axis=0)
        after = token_in + mm(gated, output_ref[...])
        hidden_in = norm_rows(after).astype(BF16)
        hidden = []
        for k in range(3):
            low = k * chunk
            loads[2 * k].wait()
            left = mm(hidden_in, trans_in_ref[:, low : low + chunk])
            loads[2 * k + 1].wait()
            right = mm(hidden_in, trans_in_ref[:, hidden_width + low : hidden_width + low + chunk])
            hidden.append((jax.nn.silu(left) * right).astype(BF16))
        hidden = jnp.concatenate(hidden, axis=1)
        loads[6].wait()
        result = (after + mm(hidden, trans_out_ref[...])).astype(BF16)
        token_out_ref[...] = result.reshape(samples, tokens, channels)
        feature_s[...] = mm(result, to_atom_ref[...]).astype(BF16).reshape(feature_s.shape)

    owner = flat_row(owner_ref)
    slots = owner.shape[1]
    onehot = (lax.broadcasted_iota(jnp.int32, (tokens, slots), 0) == owner).astype(BF16)
    final = norm_rows(mid_ref[0] + mm(onehot, feature_s[step], TN))
    high = final.astype(BF16)
    low = (final - high.astype(F32)).astype(BF16)
    terms = update_ref[...].astype(BF16)
    update = mm(terms, high, NT)
    update = update[:3] + (update[8:11] + mm(terms, low, NT)[:3])
    update = update * (owner < tokens).astype(F32)
    atom_ref[:, pl.ds(step, 1), :] = update.reshape(3, 1, slots)


def finish(
    heads, gate, tok_output, transition_in, transition_out, token_to_atom, atom_mid, atom_token, pos_update, token_in
):
    each, tokens, channels = token_in[0].shape
    samples, slots, width = atom_mid.shape
    owner = atom_token.reshape(slots // width, width)
    turned = pos_update
    whole = lambda a: pl.BlockSpec(a.shape, lambda s: (0,) * a.ndim)
    args = (heads, gate, tok_output, token_to_atom)
    return pl.pallas_call(
        finish_kernel,
        grid=(samples,),
        in_specs=[whole(a) for a in args]
        + [pl.BlockSpec((1, slots, width), lambda s: (s, 0, 0)), whole(owner), whole(turned)]
        + [pl.BlockSpec(memory_space=pl.ANY)] * 2
        + [whole(a) for a in token_in],
        out_specs=[
            pl.BlockSpec((samples, tokens, channels), lambda s: (0, 0, 0)),
            pl.BlockSpec((3, samples, slots), lambda s: (0, 0, 0)),
        ],
        out_shape=[
            jax.ShapeDtypeStruct((samples, tokens, channels), BF16),
            jax.ShapeDtypeStruct((3, samples, slots), F32),
        ],
        scratch_shapes=[
            pltpu.VMEM((samples, tokens, width), BF16),
            pltpu.VMEM(transition_in.shape, BF16),
            pltpu.VMEM(transition_out.shape, BF16),
            pltpu.SemaphoreType.DMA((7,)),
        ],
        compiler_params=params(FINISH_VMEM_LIMIT),
        cost_estimate=pl.CostEstimate(flops=8 * 10**9, bytes_accessed=10**7, transcendentals=0),
        name="finish",
    )(*args, atom_mid, owner, turned, transition_in, transition_out, *token_in)


def swap(x, axis):
    return lax.ppermute(x, axis, [(0, 1), (1, 0)])


def exchange(x, axes):
    return lax.all_to_all(x, axes, 0, 0, tiled=True)


def per_device(
    atom_cond, atom_pos, atom_token, pos_weight, atom_proj, atom_output, atom_to_token, tok_single, ada_weight,
    pair_rep, pair_weight, tok_proj, tok_output, transition_in, transition_out, token_to_atom, pos_update,
):
    tokens, channels = tok_single.shape
    heads = pair_weight.shape[1]
    samples = atom_pos.shape[0]
    pos = jnp.swapaxes(atom_pos, 0, 1)
    order = jnp.stack([lax.axis_index("xlo") * 2 + lax.axis_index("core"), lax.axis_index("xhi")]).astype(jnp.int32)
    own_bias = exchange(pair_bias(pair_rep, pair_weight), ("y", "z"))
    own_bias = own_bias.reshape(heads * tokens, own_bias.shape[2])
    mid, token_in, qkv, adapted = atom_stage(
        atom_cond, pos, atom_token, pos_weight, atom_proj, atom_output, atom_to_token, tok_single, ada_weight, tok_proj,
        heads,
    )
    own_bias, qkv = lax.optimization_barrier((own_bias, qkv))
    across = swap(own_bias, "xlo")
    near = swap(own_bias, "core")
    own = exchange(qkv, ("y", "z"))
    gate, terms = project_gate(adapted, tok_proj, pos_update)
    across, gate = lax.optimization_barrier((across, gate))
    parts = 2
    spans = samples * tokens // parts
    fars = [swap(own[:, channels // heads :, k * spans : (k + 1) * spans], "xhi") for k in range(parts)]
    biases = (own_bias, near, across, swap(across, "core"))
    running = attend(order, own, biases, samples)
    attended = None
    for k in range(parts):
        attended = attend(order, own, biases, samples, fars[k], running, k, attended)
    attended = exchange(attended, ("y", "z"))
    token_out, update = finish(
        attended, gate, tok_output, transition_in, transition_out, token_to_atom, mid, atom_token, terms, [token_in]
    )
    return token_out, jnp.swapaxes(update, 0, 1)


def solution(mesh):
    fine = Mesh(mesh.devices.reshape(2, 2, 2, 4, 4), ("xlo", "core", "xhi", "y", "z"))
    tok = ("xhi", "y", "z")
    sample = ("xlo", "core")
    return jax.shard_map(
        per_device,
        mesh=fine,
        in_specs=(
            P(tok, None), P(sample, None, tok), P(tok), P(), P(), P(), P(), P(tok, None), P(),
            P(tok, sample, None), P(), P(), P(), P(), P(), P(), P(),
        ),
        out_specs=(P(sample, tok, None), P(sample, None, tok)),
        check_vma=False,
    )
```

```python
import functools

import jax
import jax.numpy as jnp
import numpy as np
from jax import lax
from jax.experimental import pallas as pl
from jax.experimental.pallas import tpu as pltpu
from jax.sharding import Mesh, PartitionSpec as P

ATOM_HEADS = 4
QUERY_BLOCK = 32
KEY_WINDOW = 128
NORM_EPSILON = 1e-05
MASKED_SCORE = -1000000000.0
LOG2E = 1.4426950408889634
F32 = jnp.float32
BF16 = jnp.bfloat16
VMEM_LIMIT = 52 * 1024 * 1024
PAIR_VMEM_LIMIT = 60 * 1024 * 1024
ATTEND_VMEM_LIMIT = 44 * 1024 * 1024
FINISH_VMEM_LIMIT = 52 * 1024 * 1024

TN = (((0,), (0,)), ((), ()))
NT = (((1,), (1,)), ((), ()))
NN = (((1,), (0,)), ((), ()))


def flat_row(ref):
    return jnp.concatenate([ref[i : i + 1, :] for i in range(ref.shape[0])], axis=1)


def mm(a, b, dims=NN):
    return lax.dot_general(a, b, dims, preferred_element_type=F32)


def norm_rows(inputs):
    row_mean = jnp.mean(inputs, axis=-1, keepdims=True)
    centered = inputs - row_mean
    variance = jnp.mean(centered * centered, axis=-1, keepdims=True)
    return centered * lax.rsqrt(variance + NORM_EPSILON)


def params(limit=VMEM_LIMIT):
    return pltpu.CompilerParams(vmem_limit_bytes=limit)


def pair_kernel(pair_ref, weight_ref, out_ref, center_s):
    rows, cols, width = pair_ref.shape
    heads = weight_ref.shape[0]

    @pl.when(pl.program_id(0) == 0)
    def _():
        same = lax.broadcasted_iota(jnp.int32, (width, width), 0) == lax.broadcasted_iota(jnp.int32, (width, width), 1)
        center_s[...] = (same.astype(F32) - 1.0 / width).astype(BF16)

    flat = pair_ref[...].reshape(rows * cols, width)
    centered = mm(center_s[...], flat, NT)
    variance = jnp.mean(centered * centered, axis=0, keepdims=True)
    top = mm(weight_ref[...], centered.astype(BF16))
    bias = top * (lax.rsqrt(variance + NORM_EPSILON) * LOG2E)
    for h in range(heads):
        out_ref[h] = bias[h : h + 1].reshape(rows, cols).astype(BF16)


def pair_bias(pair_rep, pair_weight):
    rows, cols, width = pair_rep.shape
    heads = pair_weight.shape[1]
    step = 32
    return pl.pallas_call(
        pair_kernel,
        grid=(rows // step,),
        in_specs=[
            pl.BlockSpec((step, cols, width), lambda i: (i, 0, 0)),
            pl.BlockSpec((heads, width), lambda i: (0, 0)),
        ],
        out_specs=pl.BlockSpec((heads, step, cols), lambda i: (0, i, 0)),
        out_shape=jax.ShapeDtypeStruct((heads, rows, cols), BF16),
        scratch_shapes=[pltpu.VMEM((width, width), BF16)],
        compiler_params=params(PAIR_VMEM_LIMIT),
        cost_estimate=pl.CostEstimate(flops=10**10, bytes_accessed=10**7, transcendentals=0),
        name="pair_bias",
    )(pair_rep, pair_weight.T)


def split_three(value, order):
    first = value.astype(BF16).astype(F32)
    second = (value - first).astype(BF16).astype(F32)
    third = value - first - second
    terms = (first, second, third)
    return [terms[k] for k in order]


def atom_kernel(
    cond_ref, pos_ref, token_ref, pos_weight_ref, proj_ref, output_ref, to_token_ref, single_ref, ada_hbm, tok_proj_hbm,
    mid_ref, token_in_ref, heads_ref, adapted_ref,
    query_s, key_s, val_s, mixed_s, pos_s, weight_s, token_s, ada_ref, tok_proj_ref, sems,
):
    slots, width = cond_ref.shape
    tokens, channels = token_in_ref.shape[1:]
    heads, triple, lanes = heads_ref.shape
    sample = pl.program_id(0)
    load_ada = pltpu.make_async_copy(ada_hbm, ada_ref, sems.at[0])
    load_proj = pltpu.make_async_copy(tok_proj_hbm.at[:, pl.ds(0, 3 * channels)], tok_proj_ref, sems.at[1])
    head = width // ATOM_HEADS
    owner = flat_row(token_ref)
    count = jnp.sum((owner < tokens).astype(jnp.int32))

    @pl.when(sample == 0)
    def _():
        load_ada.start()
        load_proj.start()
        pos_s[...] = jnp.zeros_like(pos_s)
        weight_s[...] = jnp.zeros_like(weight_s)
        for k, piece in enumerate(split_three(pos_weight_ref[...], (0, 0, 0, 1, 1, 2))):
            weight_s[8 * k : 8 * k + 3, :] = piece
        val_s[:, width:] = jnp.ones((slots, width), BF16)

    position = pos_ref[:, pl.ds(sample, 1), :].reshape(3, slots)
    for k, piece in enumerate(split_three(position, (0, 1, 2, 0, 1, 0))):
        pos_s[8 * k : 8 * k + 3, :] = piece
    act = cond_ref[...].astype(F32) + mm(pos_s[...].astype(BF16), weight_s[...].astype(BF16), TN)
    normed = norm_rows(act).astype(BF16)
    projected = mm(normed, proj_ref[...])
    query_s[...] = (projected[:, :width] * (head ** (-0.5) * LOG2E)).astype(BF16)
    key_s[...] = projected[:, width : 2 * width].astype(BF16)
    val_s[:, :width] = projected[:, 2 * width :].astype(BF16)
    stacked = ATOM_HEADS * QUERY_BLOCK
    of_row = lax.broadcasted_iota(jnp.int32, (stacked, width), 0) // QUERY_BLOCK
    of_lane = lax.broadcasted_iota(jnp.int32, (stacked, width), 1) // head
    own_head = of_row == of_lane
    lane = lax.broadcasted_iota(jnp.int32, (stacked, KEY_WINDOW), 1)
    blocks = slots // QUERY_BLOCK
    group = 16
    for first in range(0, blocks, group):
        starts = [
            min(max(b * QUERY_BLOCK - (KEY_WINDOW - QUERY_BLOCK) // 2, 0), slots - KEY_WINDOW)
            for b in range(first, first + group)
        ]
        scores = []
        for k, start in enumerate(starts):
            low = (first + k) * QUERY_BLOCK
            query = query_s[low : low + QUERY_BLOCK, :]
            query = jnp.concatenate([query] * ATOM_HEADS, axis=0)
            query = jnp.where(own_head, query, jnp.zeros_like(query))
            score = mm(query, key_s[start : start + KEY_WINDOW, :], NT)
            scores.append(jnp.where(lane < count - start, score, MASKED_SCORE))
        weights = [jnp.exp2(s - jnp.max(s, axis=-1, keepdims=True)).astype(BF16) for s in scores]
        for k, start in enumerate(starts):
            low = (first + k) * QUERY_BLOCK
            summed = mm(weights[k], val_s[start : start + KEY_WINDOW, :])
            mixed = jnp.where(own_head, summed[:, :width] / summed[:, width:], 0.0)
            mixed = mixed.reshape(ATOM_HEADS, QUERY_BLOCK, width).sum(axis=0)
            mixed_s[low : low + QUERY_BLOCK, :] = mixed.astype(BF16)
    mid = act + mm(mixed_s[...], output_ref[...])
    mid_ref[0] = mid
    feature = jnp.maximum(mm(mid.astype(BF16), to_token_ref[...]), 0.0).astype(BF16)
    onehot = lax.broadcasted_iota(jnp.int32, (tokens, slots), 0) == owner
    members = jnp.sum(onehot.astype(F32), axis=1, keepdims=True)
    token_in = mm(onehot.astype(BF16), feature) / members
    token_in_ref[0] = token_in
    token_s[pl.ds(pl.multiple_of(sample * tokens, tokens), tokens), :] = norm_rows(token_in)

    @pl.when(sample == pl.num_programs(0) - 1)
    def _():
        load_ada.wait()
        load_proj.wait()
        conditioning = 1.0 + mm(single_ref[...], ada_ref[...])
        normed_tokens = token_s[...].reshape(lanes // tokens, tokens, channels)
        adapted = (normed_tokens * conditioning[None]).astype(BF16).reshape(lanes, channels)
        adapted_ref[...] = adapted
        size = triple // 3
        for part in range(3):
            rows = mm(adapted, tok_proj_ref[:, part * channels : (part + 1) * channels])
            if part == 0:
                rows = rows * (size ** (-0.5) * LOG2E)
            heads_ref[:, part * size : (part + 1) * size, :] = rows.T.astype(BF16).reshape(heads, size, lanes)


def atom_stage(
    atom_cond, atom_pos, atom_token, pos_weight, atom_proj, atom_output, atom_to_token, tok_single, ada_weight, tok_proj, heads
):
    samples = atom_pos.shape[1]
    slots, width = atom_cond.shape
    tokens, channels = tok_single.shape
    lanes = samples * tokens
    triple = 3 * channels // heads
    whole = lambda a: pl.BlockSpec(a.shape, lambda s: (0,) * a.ndim)
    atom_token = atom_token.reshape(slots // width, width)
    args = (atom_cond, atom_pos, atom_token, pos_weight, atom_proj, atom_output, atom_to_token, tok_single)
    return pl.pallas_call(
        atom_kernel,
        grid=(samples,),
        in_specs=[whole(a) for a in args] + [pl.BlockSpec(memory_space=pl.ANY)] * 2,
        out_specs=[
            pl.BlockSpec((1, slots, width), lambda s: (s, 0, 0)),
            pl.BlockSpec((1, tokens, channels), lambda s: (s, 0, 0)),
            pl.BlockSpec((heads, triple, lanes), lambda s: (0, 0, 0)),
            pl.BlockSpec((lanes, channels), lambda s: (0, 0)),
        ],
        out_shape=[
            jax.ShapeDtypeStruct((samples, slots, width), F32),
            jax.ShapeDtypeStruct((samples, tokens, channels), F32),
            jax.ShapeDtypeStruct((heads, triple, lanes), BF16),
            jax.ShapeDtypeStruct((lanes, channels), BF16),
        ],
        scratch_shapes=[
            pltpu.VMEM((slots, width), BF16),
            pltpu.VMEM((slots, width), BF16),
            pltpu.VMEM((slots, 2 * width), BF16),
            pltpu.VMEM((slots, width), BF16),
            pltpu.VMEM((48, slots), F32),
            pltpu.VMEM((48, width), F32),
            pltpu.VMEM((lanes, channels), F32),
            pltpu.VMEM((channels, channels), BF16),
            pltpu.VMEM((channels, 3 * channels), BF16),
            pltpu.SemaphoreType.DMA((2,)),
        ],
        compiler_params=params(),
        cost_estimate=pl.CostEstimate(flops=20 * 10**9, bytes_accessed=10**7, transcendentals=0),
        name="atom_stage",
    )(*args, ada_weight, tok_proj)


def gate_kernel(adapted_ref, proj_ref, update_ref, gate_ref, terms_ref):
    gate_ref[...] = jax.nn.sigmoid(mm(adapted_ref[...], proj_ref[...]))
    weight = update_ref[...]
    first = weight.astype(BF16).astype(F32)
    terms_ref[...] = jnp.zeros_like(terms_ref)
    terms_ref[0:3, :] = first
    terms_ref[8:11, :] = weight - first


def project_gate(adapted, tok_proj, pos_update):
    lanes, channels = adapted.shape
    turned = pos_update.T
    return pl.pallas_call(
        gate_kernel,
        grid=(1,),
        in_specs=[
            pl.BlockSpec((lanes, channels), lambda i: (0, 0)),
            pl.BlockSpec((channels, channels), lambda i: (0, 3)),
            pl.BlockSpec(turned.shape, lambda i: (0, 0)),
        ],
        out_specs=[
            pl.BlockSpec((lanes, channels), lambda i: (0, 0)),
            pl.BlockSpec((16, turned.shape[1]), lambda i: (0, 0)),
        ],
        out_shape=[
            jax.ShapeDtypeStruct((lanes, channels), F32),
            jax.ShapeDtypeStruct((16, turned.shape[1]), F32),
        ],
        compiler_params=params(),
        cost_estimate=pl.CostEstimate(flops=10**9, bytes_accessed=2 * 10**6, transcendentals=0),
        name="project_gate",
    )(adapted, tok_proj, turned)


def attend_kernel(last, order_ref, own_ref, *refs):
    refs, (out_ref, query_s, key_s, val_s, bias_s, sems) = refs[:-6], refs[-6:]
    heads_ref, refs = (refs[0], refs[1:]) if last else (own_ref, refs)
    bias_refs, earlier = refs[:4], refs[4:]
    sources, _, lanes = own_ref.shape
    samples, head, keys = key_s.shape
    tokens = lanes // samples
    width = val_s.shape[2]
    rows = out_ref.shape[0] * tokens if last else out_ref.shape[1]
    cols = bias_s.shape[2]
    unit = 256
    step = pl.program_id(0)
    mine = order_ref[0]
    half = 1 - order_ref[1] if last else order_ref[1]

    swapped = mine // 2 != half

    def load(p, n, other):
        place = pl.ds(pl.multiple_of(n * unit, unit), unit)
        return pltpu.make_async_copy(bias_refs[p + 2 * other].at[place], bias_s.at[p, place], sems.at[p, n])

    @pl.when((step == 0) & swapped)
    def _():
        for n in range(sources * tokens // unit):
            for p in range(2):
                load(p, n, 1).start()

    @pl.when((step == 0) & jnp.logical_not(swapped))
    def _():
        for n in range(sources * tokens // unit):
            for p in range(2):
                load(p, n, 0).start()

    @pl.when(step == 0)
    def _():
        fill = jnp.zeros((width - head, lanes), F32)
        fill_v = jnp.where(lax.broadcasted_iota(jnp.int32, (width - head, lanes), 0) == 0, 1.0, 0.0)

        def turn(block, below):
            return jnp.concatenate([block.astype(F32), below], axis=0).T.astype(BF16)

        low = 0 if last else head
        for j in range(sources):
            query = turn(own_ref[j, :head, :], fill)
            val = turn(heads_ref[j, low + head :, :], fill_v)
            for s in range(samples):
                query_s[s, j * tokens : (j + 1) * tokens, :] = query[s * tokens : (s + 1) * tokens, :head]
                val_s[s, j * tokens : (j + 1) * tokens, :] = val[s * tokens : (s + 1) * tokens]
        for j in range(0, sources, 2):
            for s in range(samples):
                pair = [heads_ref[k, low : low + head, s * tokens : (s + 1) * tokens] for k in (j, j + 1)]
                key_s[s, :, j * tokens : (j + 2) * tokens] = jnp.concatenate(pair, axis=1)

    places = [pl.ds(pl.multiple_of((mine % 2 ^ p) * cols, cols), cols) for p in range(2)]
    lane = lax.broadcasted_iota(jnp.int32, (256, width), 1)
    results = []
    jobs = [(r, s) for r in range(0, rows, unit) for s in range(samples)]

    def score(job):
        r, s = job
        query = query_s[s, pl.ds(pl.multiple_of(step * rows + r, unit), unit), :]
        block = step * (rows // unit) + r // unit
        if s == 0:
            for p in range(2):
                load(p, block, 0).wait()
        block = pl.ds(pl.multiple_of(block * unit, unit), unit)
        return [mm(query, key_s[s, :, place]) + bias_s[p, block, :].astype(F32) for p, place in enumerate(places)]

    def soften(job, scores):
        r, s = job
        top = jnp.max(jnp.maximum(*scores), axis=-1, keepdims=True)
        total = 0.0
        if last:
            before = earlier[0][s, r : r + unit]
            top_before = before[:, width - 1 :]
            top = jnp.maximum(top, top_before)
            total = before * jnp.exp2(top_before - top)
        return job, top, total, [jnp.exp2(x - top).astype(BF16) for x in scores]

    def gather(state):
        (r, s), top, total, weights = state
        for x, place in zip(weights, places):
            total = total + mm(x, val_s[s, place, :])
        if last:
            results.append(total / total[:, head : head + 1])
        else:
            out_ref[s, r : r + unit] = jnp.where(lane == width - 1, top, total)

    ahead, state = score(jobs[0]), None
    for n, job in enumerate(jobs):
        scores = ahead
        if n + 1 < len(jobs):
            ahead = score(jobs[n + 1])
        if state is not None:
            gather(state)
        state = soften(job, scores)
    gather(state)
    if last:
        for j in range(rows // tokens):
            u, low = j * tokens // unit * samples, j * tokens % unit
            block = jnp.concatenate([r[low : low + tokens] for r in results[u : u + samples]], axis=0)
            out_ref[j] = block.T[:head].astype(BF16)


def attend(order, own, biases, samples, far=None, earlier=None, part=0, result=None):
    sources, triple, lanes = own.shape
    head = triple // 3
    tokens = lanes // samples
    width = 128
    total, cols = biases[0].shape
    last = earlier is not None
    rows = 512 if last else 256
    each = far.shape[2] // tokens if last else samples
    spans = each * tokens
    before = () if result is None else (result,)
    own_spec = pl.BlockSpec((sources, triple, spans), lambda i, *_: (0, 0, part))
    bias_specs = [pl.BlockSpec(memory_space=pl.ANY)] * 4
    running = pl.BlockSpec((each, rows, width), lambda i, *_: (part, i, 0))
    if last:
        args = (own, far, *biases, earlier, *before)
        in_specs = [own_spec, pl.BlockSpec(far.shape, lambda i, *_: (0, 0, 0))] + bias_specs + [running]
        in_specs += [pl.BlockSpec(memory_space=pl.ANY)] * len(before)
        out_specs = pl.BlockSpec((rows // tokens, head, spans), lambda i, *_: (i, 0, part))
        out_shape = jax.ShapeDtypeStruct((sources, head, lanes), BF16)
    else:
        args, in_specs = (own, *biases), [own_spec] + bias_specs
        out_specs = running
        out_shape = jax.ShapeDtypeStruct((samples, total, width), F32)
    return pl.pallas_call(
        functools.partial(attend_kernel, last),
        grid_spec=pltpu.PrefetchScalarGridSpec(
            num_scalar_prefetch=1,
            grid=(total // rows,),
            in_specs=in_specs,
            out_specs=out_specs,
            scratch_shapes=[
                pltpu.VMEM((each, total, head), BF16),
                pltpu.VMEM((each, head, total), BF16),
                pltpu.VMEM((each, total, width), BF16),
                pltpu.VMEM((2, total, cols), BF16),
                pltpu.SemaphoreType.DMA((2, total // 256)),
            ],
        ),
        out_shape=out_shape,
        input_output_aliases={8: 0} if before else {},
        compiler_params=params(ATTEND_VMEM_LIMIT),
        cost_estimate=pl.CostEstimate(flops=each * 25 * 10**8, bytes_accessed=10**6, transcendentals=0),
        name="attend",
    )(order, *args)


def finish_kernel(
    heads_ref, gate_ref, output_ref, to_atom_ref, mid_ref, owner_ref, update_ref, trans_in_hbm, trans_out_hbm, *refs
):
    token_in_refs, (token_out_ref, atom_ref, feature_s, trans_in_ref, trans_out_ref, sems) = refs[:-6], refs[-6:]
    samples, tokens, channels = token_out_ref.shape
    step = pl.program_id(0)

    @pl.when(step == 0)
    def _():
        hidden_width = trans_out_ref.shape[0]
        chunk = hidden_width // 3
        loads = []
        for k in range(3):
            for n, low in enumerate((k * chunk, hidden_width + k * chunk)):
                place = pl.ds(low, chunk)
                loads.append(pltpu.make_async_copy(trans_in_hbm.at[:, place], trans_in_ref.at[:, place], sems.at[2 * k + n]))
        loads.append(pltpu.make_async_copy(trans_out_hbm, trans_out_ref, sems.at[6]))
        for load in loads:
            load.start()
        lanes = heads_ref.shape[2]
        attended = heads_ref[...].reshape(channels, lanes).astype(F32).T
        gated = (gate_ref[...] * attended).astype(BF16)
        token_in = jnp.concatenate([ref[...].reshape(-1, channels) for ref in token_in_refs], axis=0)
        after = token_in + mm(gated, output_ref[...])
        hidden_in = norm_rows(after).astype(BF16)
        hidden = []
        for k in range(3):
            low = k * chunk
            loads[2 * k].wait()
            left = mm(hidden_in, trans_in_ref[:, low : low + chunk])
            loads[2 * k + 1].wait()
            right = mm(hidden_in, trans_in_ref[:, hidden_width + low : hidden_width + low + chunk])
            hidden.append((jax.nn.silu(left) * right).astype(BF16))
        hidden = jnp.concatenate(hidden, axis=1)
        loads[6].wait()
        result = (after + mm(hidden, trans_out_ref[...])).astype(BF16)
        token_out_ref[...] = result.reshape(samples, tokens, channels)
        feature_s[...] = mm(result, to_atom_ref[...]).astype(BF16).reshape(feature_s.shape)

    owner = flat_row(owner_ref)
    slots = owner.shape[1]
    onehot = (lax.broadcasted_iota(jnp.int32, (tokens, slots), 0) == owner).astype(BF16)
    final = norm_rows(mid_ref[0] + mm(onehot, feature_s[step], TN))
    high = final.astype(BF16)
    low = (final - high.astype(F32)).astype(BF16)
    terms = update_ref[...].astype(BF16)
    update = mm(terms, high, NT)
    update = update[:3] + (update[8:11] + mm(terms, low, NT)[:3])
    update = update * (owner < tokens).astype(F32)
    atom_ref[:, pl.ds(step, 1), :] = update.reshape(3, 1, slots)


def finish(
    heads, gate, tok_output, transition_in, transition_out, token_to_atom, atom_mid, atom_token, pos_update, token_in
):
    each, tokens, channels = token_in[0].shape
    samples, slots, width = atom_mid.shape
    owner = atom_token.reshape(slots // width, width)
    turned = pos_update
    whole = lambda a: pl.BlockSpec(a.shape, lambda s: (0,) * a.ndim)
    args = (heads, gate, tok_output, token_to_atom)
    return pl.pallas_call(
        finish_kernel,
        grid=(samples,),
        in_specs=[whole(a) for a in args]
        + [pl.BlockSpec((1, slots, width), lambda s: (s, 0, 0)), whole(owner), whole(turned)]
        + [pl.BlockSpec(memory_space=pl.ANY)] * 2
        + [whole(a) for a in token_in],
        out_specs=[
            pl.BlockSpec((samples, tokens, channels), lambda s: (0, 0, 0)),
            pl.BlockSpec((3, samples, slots), lambda s: (0, 0, 0)),
        ],
        out_shape=[
            jax.ShapeDtypeStruct((samples, tokens, channels), BF16),
            jax.ShapeDtypeStruct((3, samples, slots), F32),
        ],
        scratch_shapes=[
            pltpu.VMEM((samples, tokens, width), BF16),
            pltpu.VMEM(transition_in.shape, BF16),
            pltpu.VMEM(transition_out.shape, BF16),
            pltpu.SemaphoreType.DMA((7,)),
        ],
        compiler_params=params(FINISH_VMEM_LIMIT),
        cost_estimate=pl.CostEstimate(flops=8 * 10**9, bytes_accessed=10**7, transcendentals=0),
        name="finish",
    )(*args, atom_mid, owner, turned, transition_in, transition_out, *token_in)


def swap(x, axis):
    return lax.ppermute(x, axis, [(0, 1), (1, 0)])


def exchange(x, axes):
    return lax.all_to_all(x, axes, 0, 0, tiled=True)


def per_device(
    atom_cond, atom_pos, atom_token, pos_weight, atom_proj, atom_output, atom_to_token, tok_single, ada_weight,
    pair_rep, pair_weight, tok_proj, tok_output, transition_in, transition_out, token_to_atom, pos_update,
):
    tokens, channels = tok_single.shape
    heads = pair_weight.shape[1]
    samples = atom_pos.shape[0]
    pos = jnp.swapaxes(atom_pos, 0, 1)
    order = jnp.stack([lax.axis_index("xlo") * 2 + lax.axis_index("core"), lax.axis_index("xhi")]).astype(jnp.int32)
    own_bias = exchange(pair_bias(pair_rep, pair_weight), ("y", "z"))
    own_bias = own_bias.reshape(heads * tokens, own_bias.shape[2])
    mid, token_in, qkv, adapted = atom_stage(
        atom_cond, pos, atom_token, pos_weight, atom_proj, atom_output, atom_to_token, tok_single, ada_weight, tok_proj,
        heads,
    )
    own_bias, qkv = lax.optimization_barrier((own_bias, qkv))
    across = swap(own_bias, "xlo")
    near = swap(own_bias, "core")
    own = exchange(qkv, ("y", "z"))
    gate, terms = project_gate(adapted, tok_proj, pos_update)
    across, gate = lax.optimization_barrier((across, gate))
    parts = 2
    spans = samples * tokens // parts
    fars = [swap(own[:, channels // heads :, k * spans : (k + 1) * spans], "xhi") for k in range(parts)]
    biases = (own_bias, near, across, swap(across, "core"))
    running = attend(order, own, biases, samples)
    attended = None
    for k in range(parts):
        attended = attend(order, own, biases, samples, fars[k], running, k, attended)
    attended = exchange(attended, ("y", "z"))
    token_out, update = finish(
        attended, gate, tok_output, transition_in, transition_out, token_to_atom, mid, atom_token, terms, [token_in]
    )
    return token_out, jnp.swapaxes(update, 0, 1)


def solution(mesh):
    fine = Mesh(mesh.devices.reshape(2, 2, 2, 4, 4), ("xlo", "core", "xhi", "y", "z"))
    tok = ("xhi", "y", "z")
    sample = ("xlo", "core")
    return jax.shard_map(
        per_device,
        mesh=fine,
        in_specs=(
            P(tok, None), P(sample, None, tok), P(tok), P(), P(), P(), P(), P(tok, None), P(),
            P(tok, sample, None), P(), P(), P(), P(), P(), P(), P(),
        ),
        out_specs=(P(sample, tok, None), P(sample, None, tok)),
        check_vma=False,
    )
```
